32 devices in a mesh: batch: 4 (over y, x), dir: 8 (over z, core).
Axes of the slice: x: 2, y: 2, z: 4, core: 2. Of those that a mesh axis runs over, the one named last changes fastest.
Arguments:
- embeddings: bfloat16 [128, 2048], P(('batch', 'dir')), may hold values from -13 to 13
- directions: bfloat16 [2048, 2048], P(None, 'dir'), may hold values from -0.125 to 0.125
Outputs:
- grad_embed: float32 [128, 2048], P(('batch', 'dir'))
The draws below stay inside these ranges and needn't reach their ends.
All inputs are finite; a program needn't handle non-finite values.
Results may differ from the reference program's by a relative error of at most 0.0016.
Values may be sent and summed in bfloat16 or wider, within the bound.
A program may use at most 64 MiB of HBM per device.

```python
import jax
import jax.numpy as jnp
from jax import lax

D = 2048
KNOTS = 17
DIR_DEV = 256
ROWS = 128
DIRS = 2048
N_DIR = 8


def draw_embeddings(key, part):
    row_key = jax.random.fold_in(key, 11)
    value_key = jax.random.fold_in(key, 23)
    position = jnp.arange(ROWS, dtype=jnp.float32) / (ROWS - 1)
    jitter = jnp.clip(jax.random.normal(row_key, (ROWS,), jnp.float32), -3.0, 3.0)
    scale = 0.25 * jnp.power(10.0, position) * jnp.exp(0.3 * jitter)
    values = 0.35 * jnp.clip(jax.random.normal(value_key, (ROWS, D), jnp.float32), -5.0, 5.0) + 0.3
    return (values * scale[:, None]).astype(jnp.bfloat16)


def levels(stream_key, shape, cuts, low, top_value):
    def one(axis_at, shards_of):
        draws = jax.random.uniform(jax.random.fold_in(jax.random.fold_in(stream_key, 6), axis_at), (shards_of,), jnp.float32, low / len(cuts), top_value / len(cuts))
        return jnp.repeat(jnp.exp(draws), shape[axis_at] // shards_of).reshape((-1,) + (1,) * (len(shape) - axis_at - 1))

    level = one(*cuts[0])
    for cut in cuts[1:]:
        level = level * one(*cut)
    return level


def normal_values(key, shape, spread, reach, shards=(), held_as=jnp.bfloat16):
    result = jax.random.normal(key, shape, jnp.float32) * spread
    if len(shards) > 0:
        result = levels(key, shape, shards, -0.22, 0.18) * result
    return jnp.clip(result, min=-reach, max=reach).astype(held_as)


def setup_inputs(seed: int = 0) -> dict:
    key_list = jax.random.split(jax.random.key(seed), 3)
    return {
        "embeddings": draw_embeddings(jax.random.fold_in(key_list[2], 71), 0),
        "directions": normal_values(key_list[1], (D, DIRS), D ** -0.5, 0.125, ((1, 8),)),
    }


def knot_table():
    index = jnp.arange(KNOTS, dtype=jnp.float32)
    spacing = 3.0 / (KNOTS - 1)
    knot_pos = index * spacing
    target = jnp.exp(-0.5 * knot_pos * knot_pos)
    ends = jnp.where((index == 0) | (index == KNOTS - 1), 0.5, 1.0)
    weights = ends * spacing * target
    return (knot_pos, weights, target)

def reference(embeddings, directions):
    dir_float = directions.astype(jnp.float32)
    unit = (dir_float / jnp.sqrt(lax.optimization_barrier(jnp.sum(dir_float * dir_float, axis=0, keepdims=True)) + 1e-06)).astype(jnp.bfloat16)
    blocks = unit.reshape(D, N_DIR, DIR_DEV).transpose(1, 0, 2)
    knot_pos, weights, target = knot_table()

    def one_block(total, block):
        projected = jnp.dot(embeddings, block, preferred_element_type=jnp.float32)
        angles = knot_pos[:, None, None] * projected[None]
        cosine_vals = jnp.cos(angles)
        sine_vals = jnp.sin(angles)
        cos_mean = lax.optimization_barrier(jnp.sum(cosine_vals, axis=1)) / ROWS
        sin_mean = lax.optimization_barrier(jnp.sum(sine_vals, axis=1)) / ROWS
        cos_coef = 2.0 * weights[:, None] * (cos_mean - target[:, None])
        sin_coef = 2.0 * weights[:, None] * sin_mean
        grad_proj = lax.optimization_barrier(jnp.sum(knot_pos[:, None, None] * (cosine_vals * sin_coef[:, None, :] - sine_vals * cos_coef[:, None, :]), axis=0)).astype(jnp.bfloat16)
        return (total + jnp.dot(grad_proj, block.T, preferred_element_type=jnp.float32), None)
    start_total = jnp.zeros((embeddings.shape[0], D), jnp.float32)
    grad_embed, unused = lax.scan(one_block, start_total, blocks)
    return grad_embed
```

```python
import functools

import jax
import jax.numpy as jnp
from jax import lax
from jax.experimental import pallas as pl
from jax.experimental.pallas import tpu as pltpu
from jax.sharding import PartitionSpec as P

KNOTS = 17
SPACING = 3.0 / (KNOTS - 1)
MESH = pl.DeviceIdType.MESH
TILE = 16
PARTS = 4
STEPS = 8


def sin_cos(angle):
    n = jnp.round(angle * 0.15915494309189535)
    rest = ((angle - n * 6.28125) - n * 1.9350051879882812e-3) - n * 3.019915981956753e-7
    rest = rest * 0.25
    z = rest * rest
    sine = rest + rest * z * (-1.6666654611e-1 + z * (8.3321608736e-3 - z * 1.9515295891e-4))
    cosine = 1.0 - 0.5 * z + z * z * (
        4.166664568298827e-2 + z * (-1.388731625493765e-3 + z * 2.443315711809948e-5)
    )
    for _ in range(2):
        twice = sine + sine
        sine, cosine = twice * cosine, 1.0 - twice * sine
    return sine, cosine


def kernel(
    nb, nd, emb_ref, dir_ref, out_ref,
    raw, unit, blocks, rows_f32, waves, acc, sums, coef,
    pair_out, pair_in, z_out, z_in,
    raw_sem, own_sem, e_send, e_recv, f_send, s_send, s_recv, p_send, p_recv, z_send, z_recv,
):
    chips = nd // 2
    half = chips * emb_ref.shape[0]
    per = emb_ref.shape[0]
    depth = raw.shape[0]
    total_rows = half * 2 * nb
    b, d = lax.axis_index("batch"), lax.axis_index("dir")
    chip, core = d // 2, lax.rem(d, 2)
    other = 1 - core
    partner = (b, chip * 2 + other)
    step_rows = depth // STEPS

    loads = []
    for i in range(STEPS):
        part = pl.ds(i * step_rows, step_rows)
        load = pltpu.make_async_copy(dir_ref.at[part], raw.at[part], raw_sem.at[i])
        load.start()
        loads.append(load)
    own = pltpu.make_async_copy(emb_ref, blocks.at[d], own_sem)
    own.start()

    chip_peers = [lax.rem(chip + j, chips) for j in range(1, chips)]
    batch_peers = [lax.rem(b + j, nb) for j in range(1, nb)]
    barrier = pltpu.get_barrier_semaphore()
    for c in chip_peers:
        pl.semaphore_signal(barrier, inc=1, device_id=(b, c * 2 + core), device_id_type=MESH)
    for a in batch_peers:
        pl.semaphore_signal(barrier, inc=1, device_id=(a, d), device_id_type=MESH)
    pl.semaphore_signal(barrier, inc=1, device_id=partner, device_id_type=MESH)
    pl.semaphore_wait(barrier, len(chip_peers) + len(batch_peers) + 1)

    def send_block(src, slot, sem, device):
        return pltpu.make_async_remote_copy(
            src_ref=src, dst_ref=blocks.at[slot], send_sem=sem, recv_sem=e_recv.at[slot],
            device_id=device, device_id_type=MESH,
        )

    sent = []
    for j, c in enumerate(chip_peers):
        copy = send_block(emb_ref, d, e_send.at[j], (b, c * 2 + core))
        copy.start()
        sent.append(copy)
    copy = send_block(emb_ref, d, e_send.at[chips - 1], partner)
    copy.start()
    sent.append(copy)

    square = jnp.zeros((8, raw.shape[1]), jnp.float32)
    for i in range(STEPS):
        loads[i].wait()
        value = raw[pl.ds(i * step_rows, step_rows), :].astype(jnp.float32)
        square = square + jnp.sum((value * value).reshape(step_rows // 8, 8, -1), axis=0)
    scale = 1.0 / jnp.sqrt(jnp.sum(square, axis=0, keepdims=True) + 1e-06)
    for i in range(STEPS):
        part = pl.ds(i * step_rows, step_rows)
        unit[part, :] = (raw[part, :].astype(jnp.float32) * scale).astype(jnp.bfloat16)

    own.wait()
    for j, c in enumerate(chip_peers):
        slot = c * 2 + core
        send_block(emb_ref, slot, e_send.at[j], partner).wait_recv()
        copy = send_block(blocks.at[slot], slot, f_send.at[j], partner)
        copy.start()
        sent.append(copy)

    def project(which, side):
        for c in range(chips):
            rows_f32[which, c * per:(c + 1) * per, :] = blocks[c * 2 + side].astype(jnp.float32)
        return jnp.dot(
            rows_f32[which].astype(jnp.bfloat16), unit[...], preferred_element_type=jnp.float32
        )

    def fold(value):
        return jnp.sum(value.reshape(TILE // 8, 8, -1), axis=0)

    def trig(which, projected):
        for r in range(half // TILE):
            first = which == 0 and r == 0
            at = which * half + r * TILE
            sine1, cosine1 = sin_cos(SPACING * projected[r * TILE:(r + 1) * TILE])
            powers = {1: (cosine1, sine1)}
            for k in range(1, KNOTS):
                if k > 1 and k % 2 == 0:
                    cosine, sine = powers[k // 2]
                    twice = cosine + cosine
                    powers[k] = (twice * cosine - 1.0, twice * sine)
                elif k > 1:
                    cosine, sine = powers[k - 1]
                    powers[k] = (
                        cosine * cosine1 - sine * sine1, sine * cosine1 + cosine * sine1
                    )
                for s in range(2):
                    waves[k - 1, s, at:at + TILE, :] = powers[k][s]
                    part = fold(powers[k][s])
                    acc[s, k - 1] = part if first else acc[s, k - 1] + part

    trig(0, project(0, core))
    send_rest = [lax.rem(chip + j, chips) * 2 + other for j in range(chips)]
    for slot in send_rest:
        send_block(emb_ref, slot, e_send.at[0], partner).wait_recv()
    trig(1, project(1, other))

    knots = KNOTS - 1
    for s in range(2):
        sums[b, s * knots:(s + 1) * knots, :] = jnp.sum(acc[s], axis=1)
    mine = sums.at[b]
    for j, a in enumerate(batch_peers):
        copy = pltpu.make_async_remote_copy(
            src_ref=mine, dst_ref=sums.at[b], send_sem=s_send.at[j], recv_sem=s_recv.at[b],
            device_id=(a, d), device_id_type=MESH,
        )
        copy.start()
        sent.append(copy)
    width = raw.shape[1]
    knot = lax.broadcasted_iota(jnp.int32, (knots, width), 0).astype(jnp.float32) + 1.0
    pos = knot * SPACING
    target = jnp.exp(-0.5 * pos * pos)
    ends = jnp.where(knot == float(knots), 0.5, 1.0)
    weight = 2.0 * (ends * SPACING * target)
    for j, a in enumerate(batch_peers):
        pltpu.make_async_remote_copy(
            src_ref=mine, dst_ref=sums.at[a], send_sem=s_send.at[j], recv_sem=s_recv.at[a],
            device_id=(a, d), device_id_type=MESH,
        ).wait_recv()
    total = sums[0]
    for a in range(1, nb):
        total = total + sums[a]
    mean = total * (1.0 / total_rows)
    coef[0:knots, :] = pos * (weight * (mean[0:knots] - target))
    coef[knots:2 * knots, :] = pos * (weight * mean[knots:2 * knots])
    ones = jnp.full((1, width), 1.0, jnp.float32)
    zeros = jnp.zeros((1, width), jnp.float32)
    end = 2.0 * 0.5 * SPACING
    first_term = 0.0 * (ones * (end * zeros) - zeros * (end * (ones - 1.0)))

    def grad(which):
        tiles = []
        for r in range(half // TILE):
            at = which * half + r * TILE
            value = jnp.broadcast_to(first_term, (TILE, width))
            for k in range(knots):
                value = value + (
                    waves[k, 0, at:at + TILE, :] * coef[knots + k:knots + k + 1, :]
                    - waves[k, 1, at:at + TILE, :] * coef[k:k + 1, :]
                )
            tiles.append(value)
        value = tiles[0] if len(tiles) == 1 else jnp.concatenate(tiles, axis=0)
        return value.astype(jnp.bfloat16)

    columns = depth // PARTS

    def back(value, p):
        return lax.dot_general(
            value, unit[p * columns:(p + 1) * columns, :], (((1,), (1,)), ((), ())),
            preferred_element_type=jnp.float32,
        )

    away = grad(1)
    pairs = []
    for p in range(PARTS):
        pair_out[p] = back(away, p)
        copy = pltpu.make_async_remote_copy(
            src_ref=pair_out.at[p], dst_ref=pair_in.at[p], send_sem=p_send.at[p],
            recv_sem=p_recv.at[p], device_id=partner, device_id_type=MESH,
        )
        copy.start()
        pairs.append(copy)
        sent.append(copy)
    home = grad(0)
    for p in range(PARTS):
        value = back(home, p)
        pairs[p].wait_recv()
        value = value + pair_in[p]
        for c in range(chips):
            z_out[p, c] = value[c * per:(c + 1) * per]
        for j, c in enumerate(chip_peers):
            copy = pltpu.make_async_remote_copy(
                src_ref=z_out.at[p, c], dst_ref=z_in.at[p, chip], send_sem=z_send.at[p, j],
                recv_sem=z_recv.at[p, chip], device_id=(b, c * 2 + core), device_id_type=MESH,
            )
            copy.start()
            sent.append(copy)
    for p in range(PARTS):
        value = z_out[p, chip]
        for j, c in enumerate(chip_peers):
            pltpu.make_async_remote_copy(
                src_ref=z_out.at[p, c], dst_ref=z_in.at[p, c], send_sem=z_send.at[p, j],
                recv_sem=z_recv.at[p, c], device_id=(b, c * 2 + core), device_id_type=MESH,
            ).wait_recv()
            value = value + z_in[p, c]
        out_ref[:, p * columns:(p + 1) * columns] = value
    for copy in sent:
        copy.wait_send()


def local(nb, nd, embeddings, directions):
    per, depth = embeddings.shape
    width = directions.shape[1]
    chips = nd // 2
    half = chips * per
    knots = KNOTS - 1
    columns = depth // PARTS
    f32, bf16 = jnp.float32, jnp.bfloat16
    dma = pltpu.SemaphoreType.DMA
    return pl.pallas_call(
        functools.partial(kernel, nb, nd),
        out_shape=jax.ShapeDtypeStruct((per, depth), f32),
        in_specs=[pl.BlockSpec(memory_space=pl.ANY)] * 2,
        out_specs=pl.BlockSpec(memory_space=pltpu.VMEM),
        scratch_shapes=[
            pltpu.VMEM((depth, width), bf16),
            pltpu.VMEM((depth, width), bf16),
            pltpu.VMEM((nd, per, depth), bf16),
            pltpu.VMEM((2, half, depth), f32),
            pltpu.VMEM((knots, 2, 2 * half, width), f32),
            pltpu.VMEM((2, knots, 8, width), f32),
            pltpu.VMEM((nb, 2 * knots, width), f32),
            pltpu.VMEM((2 * knots, width), f32),
            pltpu.VMEM((PARTS, half, columns), f32),
            pltpu.VMEM((PARTS, half, columns), f32),
            pltpu.VMEM((PARTS, chips, per, columns), f32),
            pltpu.VMEM((PARTS, chips, per, columns), f32),
            dma((STEPS,)),
            dma,
            dma((chips,)),
            dma((nd,)),
            dma((chips,)),
            dma((nb,)),
            dma((nb,)),
            dma((PARTS,)),
            dma((PARTS,)),
            dma((PARTS, chips)),
            dma((PARTS, chips)),
        ],
        compiler_params=pltpu.CompilerParams(
            collective_id=0, has_side_effects=True, vmem_limit_bytes=48 * 1024 * 1024
        ),
        name="sigreg_backward",
    )(embeddings, directions)


def solution(mesh):
    placed = (P(("batch", "dir"), None), P(None, "dir"))
    return jax.shard_map(
        functools.partial(local, mesh.shape["batch"], mesh.shape["dir"]),
        mesh=mesh, in_specs=placed, out_specs=P(("batch", "dir"), None), check_vma=False,
    )
```

```python
import functools

import jax
import jax.numpy as jnp
from jax import lax
from jax.experimental import pallas as pl
from jax.experimental.pallas import tpu as pltpu
from jax.sharding import PartitionSpec as P

KNOTS = 17
SPACING = 3.0 / (KNOTS - 1)
MESH = pl.DeviceIdType.MESH
TILE = 16
PARTS = 4
STEPS = 8
LIFT = 2.0 ** 50


def to_wire(value):
    value = value * LIFT
    return (value * jnp.abs(value)).astype(jnp.bfloat16)


def from_wire(value):
    value = value.astype(jnp.float32)
    return value * lax.rsqrt(jnp.maximum(jnp.abs(value), 2.0 ** -126)) * (1.0 / LIFT)


def sin_cos(angle):
    n = jnp.round(angle * 0.15915494309189535)
    rest = ((angle - n * 6.28125) - n * 1.9350051879882812e-3) - n * 3.019915981956753e-7
    rest = rest * 0.25
    z = rest * rest
    sine = rest + rest * z * (-1.6666654611e-1 + z * (8.3321608736e-3 - z * 1.9515295891e-4))
    cosine = 1.0 - 0.5 * z + z * z * (
        4.166664568298827e-2 + z * (-1.388731625493765e-3 + z * 2.443315711809948e-5)
    )
    for _ in range(2):
        twice = sine + sine
        sine, cosine = twice * cosine, 1.0 - twice * sine
    return sine, cosine


def kernel(
    nb, nd, emb_ref, dir_ref, out_ref,
    raw, unit, blocks, rows_f32, waves, acc, sums, coef,
    pair_out, pair_in, z_own, z_out, z_in,
    raw_sem, own_sem, e_send, e_recv, f_send, s_send, s_recv, p_send, p_recv, z_send, z_recv,
):
    chips = nd // 2
    half = chips * emb_ref.shape[0]
    per = emb_ref.shape[0]
    depth = raw.shape[0]
    total_rows = half * 2 * nb
    b, d = lax.axis_index("batch"), lax.axis_index("dir")
    chip, core = d // 2, lax.rem(d, 2)
    other = 1 - core
    partner = (b, chip * 2 + other)
    step_rows = depth // STEPS

    loads = []
    for i in range(STEPS):
        part = pl.ds(i * step_rows, step_rows)
        load = pltpu.make_async_copy(dir_ref.at[part], raw.at[part], raw_sem.at[i])
        load.start()
        loads.append(load)
    own = pltpu.make_async_copy(emb_ref, blocks.at[d], own_sem)
    own.start()

    chip_peers = [lax.rem(chip + j, chips) for j in range(1, chips)]
    batch_peers = [lax.rem(b + j, nb) for j in range(1, nb)]
    barrier = pltpu.get_barrier_semaphore()
    for c in chip_peers:
        pl.semaphore_signal(barrier, inc=1, device_id=(b, c * 2 + core), device_id_type=MESH)
    for a in batch_peers:
        pl.semaphore_signal(barrier, inc=1, device_id=(a, d), device_id_type=MESH)
    pl.semaphore_signal(barrier, inc=1, device_id=partner, device_id_type=MESH)
    pl.semaphore_wait(barrier, len(chip_peers) + len(batch_peers) + 1)

    def send_block(src, slot, sem, device):
        return pltpu.make_async_remote_copy(
            src_ref=src, dst_ref=blocks.at[slot], send_sem=sem, recv_sem=e_recv.at[slot],
            device_id=device, device_id_type=MESH,
        )

    sent = []
    own.wait()
    for j, c in enumerate(chip_peers):
        copy = send_block(blocks.at[d], d, e_send.at[j], (b, c * 2 + core))
        copy.start()
        sent.append(copy)
    copy = send_block(blocks.at[d], d, e_send.at[chips - 1], partner)
    copy.start()
    sent.append(copy)

    for load in loads:
        load.wait()
    width = raw.shape[1]

    def add_squares(i, square):
        part = pl.ds(pl.multiple_of(i * step_rows, step_rows), step_rows)
        value = raw[part, :].astype(jnp.float32)
        return square + jnp.sum((value * value).reshape(step_rows // 8, 8, width), axis=0)

    square = lax.fori_loop(0, STEPS, add_squares, jnp.zeros((8, width), jnp.float32))
    scale = 1.0 / jnp.sqrt(jnp.sum(square, axis=0, keepdims=True) + 1e-06)

    def normalize(i, carry):
        part = pl.ds(pl.multiple_of(i * step_rows, step_rows), step_rows)
        unit[part, :] = (raw[part, :].astype(jnp.float32) * scale).astype(jnp.bfloat16)
        return carry

    lax.fori_loop(0, STEPS, normalize, 0)

    for j, c in enumerate(chip_peers):
        slot = c * 2 + core
        send_block(emb_ref, slot, e_send.at[j], partner).wait_recv()
        copy = send_block(blocks.at[slot], slot, f_send.at[j], partner)
        copy.start()
        sent.append(copy)

    def project(which, side):
        for c in range(chips):
            rows_f32[which, c * per:(c + 1) * per, :] = blocks[c * 2 + side].astype(jnp.float32)
        return jnp.dot(
            rows_f32[which].astype(jnp.bfloat16), unit[...], preferred_element_type=jnp.float32
        )

    def fold(value):
        return jnp.sum(value.reshape(TILE // 8, 8, -1), axis=0)

    def trig(which, projected):
        for r in range(half // TILE):
            first = which == 0 and r == 0
            at = which * half + r * TILE
            sine1, cosine1 = sin_cos(SPACING * projected[r * TILE:(r + 1) * TILE])
            powers = {1: (cosine1, sine1)}
            for k in range(1, KNOTS):
                if k > 1 and k % 2 == 0:
                    cosine, sine = powers[k // 2]
                    twice = cosine + cosine
                    powers[k] = (twice * cosine - 1.0, twice * sine)
                elif k > 1:
                    cosine, sine = powers[k - 1]
                    powers[k] = (
                        cosine * cosine1 - sine * sine1, sine * cosine1 + cosine * sine1
                    )
                for s in range(2):
                    waves[k - 1, s, at:at + TILE, :] = powers[k][s]
                    part = fold(powers[k][s])
                    acc[s, k - 1] = part if first else acc[s, k - 1] + part

    trig(0, project(0, core))
    send_rest = [lax.rem(chip + j, chips) * 2 + other for j in range(chips)]
    for slot in send_rest:
        send_block(emb_ref, slot, e_send.at[0], partner).wait_recv()
    trig(1, project(1, other))

    knots = KNOTS - 1
    for s in range(2):
        sums[b, s * knots:(s + 1) * knots, :] = jnp.sum(acc[s], axis=1)
    mine = sums.at[b]
    for j, a in enumerate(batch_peers):
        copy = pltpu.make_async_remote_copy(
            src_ref=mine, dst_ref=sums.at[b], send_sem=s_send.at[j], recv_sem=s_recv.at[b],
            device_id=(a, d), device_id_type=MESH,
        )
        copy.start()
        sent.append(copy)
    knot = lax.broadcasted_iota(jnp.int32, (knots, width), 0).astype(jnp.float32) + 1.0
    pos = knot * SPACING
    target = jnp.exp(-0.5 * pos * pos)
    ends = jnp.where(knot == float(knots), 0.5, 1.0)
    weight = 2.0 * (ends * SPACING * target)
    for j, a in enumerate(batch_peers):
        pltpu.make_async_remote_copy(
            src_ref=mine, dst_ref=sums.at[a], send_sem=s_send.at[j], recv_sem=s_recv.at[a],
            device_id=(a, d), device_id_type=MESH,
        ).wait_recv()
    total = sums[0]
    for a in range(1, nb):
        total = total + sums[a]
    mean = total * (1.0 / total_rows)
    coef[0:knots, :] = pos * (weight * (mean[0:knots] - target))
    coef[knots:2 * knots, :] = pos * (weight * mean[knots:2 * knots])
    ones = jnp.full((1, width), 1.0, jnp.float32)
    zeros = jnp.zeros((1, width), jnp.float32)
    end = 2.0 * 0.5 * SPACING
    first_term = 0.0 * (ones * (end * zeros) - zeros * (end * (ones - 1.0)))

    def grad(which):
        tiles = []
        for r in range(half // TILE):
            at = which * half + r * TILE
            value = jnp.broadcast_to(first_term, (TILE, width))
            for k in range(knots):
                value = value + (
                    waves[k, 0, at:at + TILE, :] * coef[knots + k:knots + k + 1, :]
                    - waves[k, 1, at:at + TILE, :] * coef[k:k + 1, :]
                )
            tiles.append(value)
        value = tiles[0] if len(tiles) == 1 else jnp.concatenate(tiles, axis=0)
        return value.astype(jnp.bfloat16)

    columns = depth // PARTS

    def back(value, p):
        return lax.dot_general(
            value, unit[p * columns:(p + 1) * columns, :], (((1,), (1,)), ((), ())),
            preferred_element_type=jnp.float32,
        )

    away = grad(1)
    pairs = []
    for p in range(PARTS):
        pair_out[p] = back(away, p)
        copy = pltpu.make_async_remote_copy(
            src_ref=pair_out.at[p], dst_ref=pair_in.at[p], send_sem=p_send.at[p],
            recv_sem=p_recv.at[p], device_id=partner, device_id_type=MESH,
        )
        copy.start()
        pairs.append(copy)
        sent.append(copy)
    home = grad(0)
    for p in range(PARTS):
        value = back(home, p)
        pairs[p].wait_recv()
        value = value + pair_in[p]
        for c in range(chips):
            z_own[p, c] = value[c * per:(c + 1) * per]
            z_out[p, c] = to_wire(value[c * per:(c + 1) * per])
        for j, c in enumerate(chip_peers):
            copy = pltpu.make_async_remote_copy(
                src_ref=z_out.at[p, c], dst_ref=z_in.at[p, chip], send_sem=z_send.at[p, j],
                recv_sem=z_recv.at[p, chip], device_id=(b, c * 2 + core), device_id_type=MESH,
            )
            copy.start()
            sent.append(copy)
    for p in range(PARTS):
        value = z_own[p, chip]
        for j, c in enumerate(chip_peers):
            pltpu.make_async_remote_copy(
                src_ref=z_out.at[p, c], dst_ref=z_in.at[p, c], send_sem=z_send.at[p, j],
                recv_sem=z_recv.at[p, c], device_id=(b, c * 2 + core), device_id_type=MESH,
            ).wait_recv()
            value = value + from_wire(z_in[p, c])
        out_ref[:, p * columns:(p + 1) * columns] = value
    for copy in sent:
        copy.wait_send()


def local(nb, nd, embeddings, directions):
    per, depth = embeddings.shape
    width = directions.shape[1]
    chips = nd // 2
    half = chips * per
    knots = KNOTS - 1
    columns = depth // PARTS
    f32, bf16 = jnp.float32, jnp.bfloat16
    dma = pltpu.SemaphoreType.DMA
    return pl.pallas_call(
        functools.partial(kernel, nb, nd),
        out_shape=jax.ShapeDtypeStruct((per, depth), f32),
        in_specs=[pl.BlockSpec(memory_space=pltpu.HBM)] * 2,
        out_specs=pl.BlockSpec(memory_space=pltpu.VMEM),
        scratch_shapes=[
            pltpu.VMEM((depth, width), bf16),
            pltpu.VMEM((depth, width), bf16),
            pltpu.VMEM((nd, per, depth), bf16),
            pltpu.VMEM((2, half, depth), f32),
            pltpu.VMEM((knots, 2, 2 * half, width), f32),
            pltpu.VMEM((2, knots, 8, width), f32),
            pltpu.VMEM((nb, 2 * knots, width), f32),
            pltpu.VMEM((2 * knots, width), f32),
            pltpu.VMEM((PARTS, half, columns), f32),
            pltpu.VMEM((PARTS, half, columns), f32),
            pltpu.VMEM((PARTS, chips, per, columns), f32),
            pltpu.VMEM((PARTS, chips, per, columns), bf16),
            pltpu.VMEM((PARTS, chips, per, columns), bf16),
            dma((STEPS,)),
            dma,
            dma((chips,)),
            dma((nd,)),
            dma((chips,)),
            dma((nb,)),
            dma((nb,)),
            dma((PARTS,)),
            dma((PARTS,)),
            dma((PARTS, chips)),
            dma((PARTS, chips)),
        ],
        compiler_params=pltpu.CompilerParams(
            collective_id=0, has_side_effects=True, vmem_limit_bytes=64 * 1024 * 1024
        ),
        name="sigreg_backward",
    )(embeddings, directions)


def solution(mesh):
    placed = (P(("batch", "dir"), None), P(None, "dir"))
    return jax.shard_map(
        functools.partial(local, mesh.shape["batch"], mesh.shape["dir"]),
        mesh=mesh, in_specs=placed, out_specs=P(("batch", "dir"), None), check_vma=False,
    )
```

```python
import functools

import jax
import jax.numpy as jnp
from jax import lax
from jax.experimental import pallas as pl
from jax.experimental.pallas import tpu as pltpu
from jax.sharding import PartitionSpec as P

KNOTS = 17
SPACING = 3.0 / (KNOTS - 1)
MESH = pl.DeviceIdType.MESH
TILE = 16
PARTS = 4
GROUPS = 2
STEPS = 8
LIFT = 2.0 ** 50


def to_wire(value):
    value = value * LIFT
    return (value * jnp.abs(value)).astype(jnp.bfloat16)


def from_wire(value):
    value = value.astype(jnp.float32)
    return value * lax.rsqrt(jnp.maximum(jnp.abs(value), 2.0 ** -126)) * (1.0 / LIFT)


def sin_cos(angle):
    n = jnp.round(angle * 0.15915494309189535)
    rest = ((angle - n * 6.28125) - n * 1.9350051879882812e-3) - n * 3.019915981956753e-7
    rest = rest * 0.25
    z = rest * rest
    sine = rest + rest * z * (-1.6666654611e-1 + z * (8.3321608736e-3 - z * 1.9515295891e-4))
    cosine = 1.0 - 0.5 * z + z * z * (
        4.166664568298827e-2 + z * (-1.388731625493765e-3 + z * 2.443315711809948e-5)
    )
    for _ in range(2):
        twice = sine + sine
        sine, cosine = twice * cosine, 1.0 - twice * sine
    return sine, cosine


def kernel(
    nb, nd, emb_ref, dir_ref, out_ref,
    raw, unit, blocks, rows_f32, waves, acc, sums, coef, grads,
    pair_out, pair_in, z_own, z_out, z_in,
    raw_sem, own_sem, e_send, e_recv, f_send, s_send, s_recv, p_send, p_recv, z_send, z_recv,
):
    chips = nd // 2
    half = chips * emb_ref.shape[0]
    per = emb_ref.shape[0]
    depth = raw.shape[0]
    total_rows = half * 2 * nb
    b, d = lax.axis_index("batch"), lax.axis_index("dir")
    chip, core = d // 2, lax.rem(d, 2)
    other = 1 - core
    partner = (b, chip * 2 + other)
    step_rows = depth // STEPS

    loads = []
    for i in range(STEPS):
        part = pl.ds(i * step_rows, step_rows)
        load = pltpu.make_async_copy(dir_ref.at[part], raw.at[part], raw_sem.at[i])
        load.start()
        loads.append(load)
    own = pltpu.make_async_copy(emb_ref, blocks.at[d], own_sem)
    own.start()

    chip_peers = [lax.rem(chip + j, chips) for j in range(1, chips)]
    batch_peers = [lax.rem(b + j, nb) for j in range(1, nb)]
    barrier = pltpu.get_barrier_semaphore()
    for c in chip_peers:
        pl.semaphore_signal(barrier, inc=1, device_id=(b, c * 2 + core), device_id_type=MESH)
    for a in batch_peers:
        pl.semaphore_signal(barrier, inc=1, device_id=(a, d), device_id_type=MESH)
    pl.semaphore_signal(barrier, inc=1, device_id=partner, device_id_type=MESH)
    pl.semaphore_wait(barrier, len(chip_peers) + len(batch_peers) + 1)

    def send_block(src, slot, sem, device):
        return pltpu.make_async_remote_copy(
            src_ref=src, dst_ref=blocks.at[slot], send_sem=sem, recv_sem=e_recv.at[slot],
            device_id=device, device_id_type=MESH,
        )

    sent = []
    own.wait()
    for j, c in enumerate(chip_peers):
        copy = send_block(blocks.at[d], d, e_send.at[j], (b, c * 2 + core))
        copy.start()
        sent.append(copy)
    copy = send_block(blocks.at[d], d, e_send.at[chips - 1], partner)
    copy.start()
    sent.append(copy)

    for load in loads:
        load.wait()
    width = raw.shape[1]

    def add_squares(i, square):
        part = pl.ds(pl.multiple_of(i * step_rows, step_rows), step_rows)
        value = raw[part, :].astype(jnp.float32)
        return square + jnp.sum((value * value).reshape(step_rows // 8, 8, width), axis=0)

    square = lax.fori_loop(0, STEPS, add_squares, jnp.zeros((8, width), jnp.float32))
    scale = 1.0 / jnp.sqrt(jnp.sum(square, axis=0, keepdims=True) + 1e-06)

    def normalize(i, carry):
        part = pl.ds(pl.multiple_of(i * step_rows, step_rows), step_rows)
        unit[part, :] = (raw[part, :].astype(jnp.float32) * scale).astype(jnp.bfloat16)
        return carry

    lax.fori_loop(0, STEPS, normalize, 0)

    for j, c in enumerate(chip_peers):
        slot = c * 2 + core
        send_block(emb_ref, slot, e_send.at[j], partner).wait_recv()
        copy = send_block(blocks.at[slot], slot, f_send.at[j], partner)
        copy.start()
        sent.append(copy)

    wide = width // GROUPS
    knots = KNOTS - 1

    def gather_rows(which, side):
        for c in range(chips):
            rows_f32[which, c * per:(c + 1) * per, :] = blocks[c * 2 + side].astype(jnp.float32)
        return rows_f32[which].astype(jnp.bfloat16)

    def project(rows, g):
        return jnp.dot(
            rows, unit[:, g * wide:(g + 1) * wide], preferred_element_type=jnp.float32
        )

    def fold(value):
        return jnp.sum(value.reshape(TILE // 8, 8, -1), axis=0)

    def trig(which, projected, g):
        lanes = pl.ds(g * wide, wide)
        for r in range(half // TILE):
            first = which == 0 and r == 0
            at = which * half + r * TILE
            sine1, cosine1 = sin_cos(SPACING * projected[r * TILE:(r + 1) * TILE])
            powers = {1: (cosine1, sine1)}
            for k in range(1, KNOTS):
                if k > 1 and k % 2 == 0:
                    cosine, sine = powers[k // 2]
                    twice = cosine + cosine
                    powers[k] = (twice * cosine - 1.0, twice * sine)
                elif k > 1:
                    cosine, sine = powers[k - 1]
                    powers[k] = (
                        cosine * cosine1 - sine * sine1, sine * cosine1 + cosine * sine1
                    )
                for s in range(2):
                    waves[k - 1, s, at:at + TILE, lanes] = powers[k][s]
                    part = fold(powers[k][s])
                    rows = pl.ds((s * knots + k - 1) * 8, 8)
                    acc[g, rows, :] = part if first else acc[g, rows, :] + part

    home_rows = gather_rows(0, core)
    for g in range(GROUPS):
        trig(0, project(home_rows, g), g)
    send_rest = [lax.rem(chip + j, chips) * 2 + other for j in range(chips)]
    for slot in send_rest:
        send_block(emb_ref, slot, e_send.at[0], partner).wait_recv()
    away_rows = gather_rows(1, other)

    def send_sums(g, j, a, slot):
        return pltpu.make_async_remote_copy(
            src_ref=sums.at[g, b], dst_ref=sums.at[g, slot], send_sem=s_send.at[g, j],
            recv_sem=s_recv.at[g, slot], device_id=(a, d), device_id_type=MESH,
        )

    for g in range(GROUPS):
        trig(1, project(away_rows, g), g)
        value = acc[g, pl.ds(0, 2 * knots, stride=8), :]
        for i in range(1, 8):
            value = value + acc[g, pl.ds(i, 2 * knots, stride=8), :]
        sums[g, b] = value
        for j, a in enumerate(batch_peers):
            copy = send_sums(g, j, a, b)
            copy.start()
            sent.append(copy)
    knot = lax.broadcasted_iota(jnp.int32, (knots, wide), 0).astype(jnp.float32) + 1.0
    pos = knot * SPACING
    target = jnp.exp(-0.5 * pos * pos)
    ends = jnp.where(knot == float(knots), 0.5, 1.0)
    weight = 2.0 * (ends * SPACING * target)

    def coefficients(g):
        for j, a in enumerate(batch_peers):
            send_sums(g, j, a, a).wait_recv()
        total = sums[g, 0]
        for a in range(1, nb):
            total = total + sums[g, a]
        mean = total * (1.0 / total_rows)
        coef[g, 0:knots, :] = pos * (weight * (mean[0:knots] - target))
        coef[g, knots:2 * knots, :] = pos * (weight * mean[knots:2 * knots])

    ones = jnp.full((1, wide), 1.0, jnp.float32)
    zeros = jnp.zeros((1, wide), jnp.float32)
    end = 2.0 * 0.5 * SPACING
    first_term = 0.0 * (ones * (end * zeros) - zeros * (end * (ones - 1.0)))

    def grad(which, g):
        lanes = pl.ds(g * wide, wide)
        for r in range(half // TILE):
            at = which * half + r * TILE
            value = jnp.broadcast_to(first_term, (TILE, wide))
            for k in range(knots):
                value = value + (
                    waves[k, 0, at:at + TILE, lanes] * coef[g, knots + k:knots + k + 1, :]
                    - waves[k, 1, at:at + TILE, lanes] * coef[g, k:k + 1, :]
                )
            grads[at:at + TILE, lanes] = value.astype(jnp.bfloat16)

    columns = depth // PARTS

    def back(value, p):
        return lax.dot_general(
            value, unit[p * columns:(p + 1) * columns, :], (((1,), (1,)), ((), ())),
            preferred_element_type=jnp.float32,
        )

    for g in range(GROUPS):
        coefficients(g)
        grad(1, g)
        if g + 1 < GROUPS:
            grad(0, g)
    away = grads[half:2 * half, :]
    pairs = []
    for p in range(PARTS):
        pair_out[p] = back(away, p)
        copy = pltpu.make_async_remote_copy(
            src_ref=pair_out.at[p], dst_ref=pair_in.at[p], send_sem=p_send.at[p],
            recv_sem=p_recv.at[p], device_id=partner, device_id_type=MESH,
        )
        copy.start()
        pairs.append(copy)
        sent.append(copy)
    grad(0, GROUPS - 1)
    home = grads[0:half, :]
    for p in range(PARTS):
        value = back(home, p)
        pairs[p].wait_recv()
        value = value + pair_in[p]
        for c in range(chips):
            z_own[p, c] = value[c * per:(c + 1) * per]
            z_out[p, c] = to_wire(value[c * per:(c + 1) * per])
        for j, c in enumerate(chip_peers):
            copy = pltpu.make_async_remote_copy(
                src_ref=z_out.at[p, c], dst_ref=z_in.at[p, chip], send_sem=z_send.at[p, j],
                recv_sem=z_recv.at[p, chip], device_id=(b, c * 2 + core), device_id_type=MESH,
            )
            copy.start()
            sent.append(copy)
    for p in range(PARTS):
        value = z_own[p, chip]
        for j, c in enumerate(chip_peers):
            pltpu.make_async_remote_copy(
                src_ref=z_out.at[p, c], dst_ref=z_in.at[p, c], send_sem=z_send.at[p, j],
                recv_sem=z_recv.at[p, c], device_id=(b, c * 2 + core), device_id_type=MESH,
            ).wait_recv()
            value = value + from_wire(z_in[p, c])
        out_ref[:, p * columns:(p + 1) * columns] = value
    for copy in sent:
        copy.wait_send()


def local(nb, nd, embeddings, directions):
    per, depth = embeddings.shape
    width = directions.shape[1]
    chips = nd // 2
    half = chips * per
    knots = KNOTS - 1
    columns = depth // PARTS
    wide = width // GROUPS
    f32, bf16 = jnp.float32, jnp.bfloat16
    dma = pltpu.SemaphoreType.DMA
    return pl.pallas_call(
        functools.partial(kernel, nb, nd),
        out_shape=jax.ShapeDtypeStruct((per, depth), f32),
        in_specs=[pl.BlockSpec(memory_space=pltpu.HBM)] * 2,
        out_specs=pl.BlockSpec(memory_space=pltpu.VMEM),
        scratch_shapes=[
            pltpu.VMEM((depth, width), bf16),
            pltpu.VMEM((depth, width), bf16),
            pltpu.VMEM((nd, per, depth), bf16),
            pltpu.VMEM((2, half, depth), f32),
            pltpu.VMEM((knots, 2, 2 * half, width), f32),
            pltpu.VMEM((GROUPS, 2 * knots * 8, wide), f32),
            pltpu.VMEM((GROUPS, nb, 2 * knots, wide), f32),
            pltpu.VMEM((GROUPS, 2 * knots, wide), f32),
            pltpu.VMEM((2 * half, width), bf16),
            pltpu.VMEM((PARTS, half, columns), f32),
            pltpu.VMEM((PARTS, half, columns), f32),
            pltpu.VMEM((PARTS, chips, per, columns), f32),
            pltpu.VMEM((PARTS, chips, per, columns), bf16),
            pltpu.VMEM((PARTS, chips, per, columns), bf16),
            dma((STEPS,)),
            dma,
            dma((chips,)),
            dma((nd,)),
            dma((chips,)),
            dma((GROUPS, nb)),
            dma((GROUPS, nb)),
            dma((PARTS,)),
            dma((PARTS,)),
            dma((PARTS, chips)),
            dma((PARTS, chips)),
        ],
        compiler_params=pltpu.CompilerParams(
            collective_id=0, has_side_effects=True, vmem_limit_bytes=64 * 1024 * 1024
        ),
        name="sigreg_backward",
    )(embeddings, directions)


def solution(mesh):
    placed = (P(("batch", "dir"), None), P(None, "dir"))
    return jax.shard_map(
        functools.partial(local, mesh.shape["batch"], mesh.shape["dir"]),
        mesh=mesh, in_specs=placed, out_specs=P(("batch", "dir"), None), check_vma=False,
    )
```

```python
import functools

import jax
import jax.numpy as jnp
from jax import lax
from jax.experimental import pallas as pl
from jax.experimental.pallas import tpu as pltpu
from jax.sharding import PartitionSpec as P

KNOTS = 17
SPACING = 3.0 / (KNOTS - 1)
MESH = pl.DeviceIdType.MESH
TILE = 16
PARTS = 4
GROUPS = 2
STEPS = 8
LIFT = 2.0 ** 50


def to_wire(value):
    value = value * LIFT
    return (value * jnp.abs(value)).astype(jnp.bfloat16)


def from_wire(value):
    value = value.astype(jnp.float32)
    return value * lax.rsqrt(jnp.maximum(jnp.abs(value), 2.0 ** -126)) * (1.0 / LIFT)


def sin_cos(angle):
    n = jnp.round(angle * 0.15915494309189535)
    rest = ((angle - n * 6.28125) - n * 1.9350051879882812e-3) - n * 3.019915981956753e-7
    rest = rest * 0.25
    z = rest * rest
    sine = rest + rest * z * (-1.6666654611e-1 + z * (8.3321608736e-3 - z * 1.9515295891e-4))
    cosine = 1.0 - 0.5 * z + z * z * (
        4.166664568298827e-2 + z * (-1.388731625493765e-3 + z * 2.443315711809948e-5)
    )
    for _ in range(2):
        twice = sine + sine
        sine, cosine = twice * cosine, 1.0 - twice * sine
    return sine, cosine


def kernel(
    nb, nd, emb_ref, dir_ref, out_ref,
    raw, unit, blocks, rows_f32, waves, acc, sums, coef, grads,
    kept, pair_out, pair_in, z_own, z_out, z_in,
    raw_sem, own_sem, e_send, e_recv, f_send, s_send, s_recv, p_send, p_recv, z_send, z_recv,
):
    chips = nd // 2
    half = chips * emb_ref.shape[0]
    per = emb_ref.shape[0]
    depth = raw.shape[0]
    total_rows = half * 2 * nb
    b, d = lax.axis_index("batch"), lax.axis_index("dir")
    chip, core = d // 2, lax.rem(d, 2)
    other = 1 - core
    partner = (b, chip * 2 + other)
    step_rows = depth // STEPS

    loads = []
    for i in range(STEPS):
        part = pl.ds(i * step_rows, step_rows)
        load = pltpu.make_async_copy(dir_ref.at[part], raw.at[part], raw_sem.at[i])
        load.start()
        loads.append(load)
    own = pltpu.make_async_copy(emb_ref, blocks.at[d], own_sem)
    own.start()

    chip_peers = [lax.rem(chip + j, chips) for j in range(1, chips)]
    batch_peers = [lax.rem(b + j, nb) for j in range(1, nb)]
    barrier = pltpu.get_barrier_semaphore()
    for c in chip_peers:
        pl.semaphore_signal(barrier, inc=1, device_id=(b, c * 2 + core), device_id_type=MESH)
    for a in batch_peers:
        pl.semaphore_signal(barrier, inc=1, device_id=(a, d), device_id_type=MESH)
    pl.semaphore_signal(barrier, inc=1, device_id=partner, device_id_type=MESH)
    pl.semaphore_wait(barrier, len(chip_peers) + len(batch_peers) + 1)

    def send_block(src, slot, sem, device):
        return pltpu.make_async_remote_copy(
            src_ref=src, dst_ref=blocks.at[slot], send_sem=sem, recv_sem=e_recv.at[slot],
            device_id=device, device_id_type=MESH,
        )

    sent = []
    own.wait()
    for j, c in enumerate(chip_peers):
        copy = send_block(blocks.at[d], d, e_send.at[j], (b, c * 2 + core))
        copy.start()
        sent.append(copy)
    copy = send_block(blocks.at[d], d, e_send.at[chips - 1], partner)
    copy.start()
    sent.append(copy)

    for load in loads:
        load.wait()
    width = raw.shape[1]

    def add_squares(i, square):
        part = pl.ds(pl.multiple_of(i * step_rows, step_rows), step_rows)
        value = raw[part, :].astype(jnp.float32)
        return square + jnp.sum((value * value).reshape(step_rows // 8, 8, width), axis=0)

    square = lax.fori_loop(0, STEPS, add_squares, jnp.zeros((8, width), jnp.float32))
    scale = 1.0 / jnp.sqrt(jnp.sum(square, axis=0, keepdims=True) + 1e-06)

    def normalize(i, carry):
        part = pl.ds(pl.multiple_of(i * step_rows, step_rows), step_rows)
        unit[part, :] = (raw[part, :].astype(jnp.float32) * scale).astype(jnp.bfloat16)
        return carry

    lax.fori_loop(0, STEPS, normalize, 0)

    for j, c in enumerate(chip_peers):
        slot = c * 2 + core
        send_block(emb_ref, slot, e_send.at[j], partner).wait_recv()
        copy = send_block(blocks.at[slot], slot, f_send.at[j], partner)
        copy.start()
        sent.append(copy)

    wide = width // GROUPS
    knots = KNOTS - 1

    def gather_rows(which, side):
        for c in range(chips):
            rows_f32[which, c * per:(c + 1) * per, :] = blocks[c * 2 + side].astype(jnp.float32)
        return rows_f32[which].astype(jnp.bfloat16)

    def project(rows, g):
        return jnp.dot(
            rows, unit[:, g * wide:(g + 1) * wide], preferred_element_type=jnp.float32
        )

    def fold(value):
        return jnp.sum(value.reshape(TILE // 8, 8, -1), axis=0)

    def trig(which, projected, g):
        lanes = pl.ds(g * wide, wide)
        for r in range(half // TILE):
            first = which == 0 and r == 0
            at = which * half + r * TILE
            sine1, cosine1 = sin_cos(SPACING * projected[r * TILE:(r + 1) * TILE])
            powers = {1: (cosine1, sine1)}
            for k in range(1, KNOTS):
                if k > 1 and k % 2 == 0:
                    cosine, sine = powers[k // 2]
                    twice = cosine + cosine
                    powers[k] = (twice * cosine - 1.0, twice * sine)
                elif k > 1:
                    cosine, sine = powers[k - 1]
                    powers[k] = (
                        cosine * cosine1 - sine * sine1, sine * cosine1 + cosine * sine1
                    )
                for s in range(2):
                    waves[k - 1, s, at:at + TILE, lanes] = powers[k][s]
                    part = fold(powers[k][s])
                    rows = pl.ds((s * knots + k - 1) * 8, 8)
                    acc[g, rows, :] = part if first else acc[g, rows, :] + part

    home_rows = gather_rows(0, core)
    for g in range(GROUPS):
        trig(0, project(home_rows, g), g)
    send_rest = [lax.rem(chip + j, chips) * 2 + other for j in range(chips)]
    for slot in send_rest:
        send_block(emb_ref, slot, e_send.at[0], partner).wait_recv()
    away_rows = gather_rows(1, other)

    def send_sums(g, j, a, slot):
        return pltpu.make_async_remote_copy(
            src_ref=sums.at[g, b], dst_ref=sums.at[g, slot], send_sem=s_send.at[g, j],
            recv_sem=s_recv.at[g, slot], device_id=(a, d), device_id_type=MESH,
        )

    for g in range(GROUPS):
        trig(1, project(away_rows, g), g)
        value = acc[g, pl.ds(0, 2 * knots, stride=8), :]
        for i in range(1, 8):
            value = value + acc[g, pl.ds(i, 2 * knots, stride=8), :]
        sums[g, b] = value
        for j, a in enumerate(batch_peers):
            copy = send_sums(g, j, a, b)
            copy.start()
            sent.append(copy)
    knot = lax.broadcasted_iota(jnp.int32, (knots, wide), 0).astype(jnp.float32) + 1.0
    pos = knot * SPACING
    target = jnp.exp(-0.5 * pos * pos)
    ends = jnp.where(knot == float(knots), 0.5, 1.0)
    weight = 2.0 * (ends * SPACING * target)

    def coefficients(g):
        for j, a in enumerate(batch_peers):
            send_sums(g, j, a, a).wait_recv()
        total = sums[g, 0]
        for a in range(1, nb):
            total = total + sums[g, a]
        mean = total * (1.0 / total_rows)
        coef[g, 0:knots, :] = pos * (weight * (mean[0:knots] - target))
        coef[g, knots:2 * knots, :] = pos * (weight * mean[knots:2 * knots])

    ones = jnp.full((1, wide), 1.0, jnp.float32)
    zeros = jnp.zeros((1, wide), jnp.float32)
    end = 2.0 * 0.5 * SPACING
    first_term = 0.0 * (ones * (end * zeros) - zeros * (end * (ones - 1.0)))

    def grad(which, g):
        lanes = pl.ds(g * wide, wide)
        for r in range(half // TILE):
            at = which * half + r * TILE
            value = jnp.broadcast_to(first_term, (TILE, wide))
            for k in range(knots):
                value = value + (
                    waves[k, 0, at:at + TILE, lanes] * coef[g, knots + k:knots + k + 1, :]
                    - waves[k, 1, at:at + TILE, lanes] * coef[g, k:k + 1, :]
                )
            grads[at:at + TILE, lanes] = value.astype(jnp.bfloat16)

    columns = depth // PARTS

    def back(value, p):
        return lax.dot_general(
            value, unit[p * columns:(p + 1) * columns, :], (((1,), (1,)), ((), ())),
            preferred_element_type=jnp.float32,
        )

    for g in range(GROUPS):
        coefficients(g)
        for which in range(2):
            grad(which, g)
    both = grads[...]
    pairs = []
    for p in range(PARTS):
        value = back(both, p)
        kept[p] = value[0:half]
        pair_out[p] = value[half:2 * half]
        copy = pltpu.make_async_remote_copy(
            src_ref=pair_out.at[p], dst_ref=pair_in.at[p], send_sem=p_send.at[p],
            recv_sem=p_recv.at[p], device_id=partner, device_id_type=MESH,
        )
        copy.start()
        pairs.append(copy)
        sent.append(copy)
    for p in range(PARTS):
        pairs[p].wait_recv()
        value = kept[p] + pair_in[p]
        for c in range(chips):
            z_own[p, c] = value[c * per:(c + 1) * per]
            z_out[p, c] = to_wire(value[c * per:(c + 1) * per])
        for j, c in enumerate(chip_peers):
            copy = pltpu.make_async_remote_copy(
                src_ref=z_out.at[p, c], dst_ref=z_in.at[p, chip], send_sem=z_send.at[p, j],
                recv_sem=z_recv.at[p, chip], device_id=(b, c * 2 + core), device_id_type=MESH,
            )
            copy.start()
            sent.append(copy)
    for p in range(PARTS):
        value = z_own[p, chip]
        for j, c in enumerate(chip_peers):
            pltpu.make_async_remote_copy(
                src_ref=z_out.at[p, c], dst_ref=z_in.at[p, c], send_sem=z_send.at[p, j],
                recv_sem=z_recv.at[p, c], device_id=(b, c * 2 + core), device_id_type=MESH,
            ).wait_recv()
            value = value + from_wire(z_in[p, c])
        out_ref[:, p * columns:(p + 1) * columns] = value
    for copy in sent:
        copy.wait_send()


def local(nb, nd, embeddings, directions):
    per, depth = embeddings.shape
    width = directions.shape[1]
    chips = nd // 2
    half = chips * per
    knots = KNOTS - 1
    columns = depth // PARTS
    wide = width // GROUPS
    f32, bf16 = jnp.float32, jnp.bfloat16
    dma = pltpu.SemaphoreType.DMA
    return pl.pallas_call(
        functools.partial(kernel, nb, nd),
        out_shape=jax.ShapeDtypeStruct((per, depth), f32),
        in_specs=[pl.BlockSpec(memory_space=pltpu.HBM)] * 2,
        out_specs=pl.BlockSpec(memory_space=pltpu.VMEM),
        scratch_shapes=[
            pltpu.VMEM((depth, width), bf16),
            pltpu.VMEM((depth, width), bf16),
            pltpu.VMEM((nd, per, depth), bf16),
            pltpu.VMEM((2, half, depth), f32),
            pltpu.VMEM((knots, 2, 2 * half, width), f32),
            pltpu.VMEM((GROUPS, 2 * knots * 8, wide), f32),
            pltpu.VMEM((GROUPS, nb, 2 * knots, wide), f32),
            pltpu.VMEM((GROUPS, 2 * knots, wide), f32),
            pltpu.VMEM((2 * half, width), bf16),
            pltpu.VMEM((PARTS, half, columns), f32),
            pltpu.VMEM((PARTS, half, columns), f32),
            pltpu.VMEM((PARTS, half, columns), f32),
            pltpu.VMEM((PARTS, chips, per, columns), f32),
            pltpu.VMEM((PARTS, chips, per, columns), bf16),
            pltpu.VMEM((PARTS, chips, per, columns), bf16),
            dma((STEPS,)),
            dma,
            dma((chips,)),
            dma((nd,)),
            dma((chips,)),
            dma((GROUPS, nb)),
            dma((GROUPS, nb)),
            dma((PARTS,)),
            dma((PARTS,)),
            dma((PARTS, chips)),
            dma((PARTS, chips)),
        ],
        compiler_params=pltpu.CompilerParams(
            collective_id=0, has_side_effects=True, vmem_limit_bytes=56 * 1000 * 1000
        ),
        name="sigreg_backward",
    )(embeddings, directions)


def solution(mesh):
    placed = (P(("batch", "dir"), None), P(None, "dir"))
    return jax.shard_map(
        functools.partial(local, mesh.shape["batch"], mesh.shape["dir"]),
        mesh=mesh, in_specs=placed, out_specs=P(("batch", "dir"), None), check_vma=False,
    )
```

```python
import functools

import jax
import jax.numpy as jnp
from jax import lax
from jax.experimental import pallas as pl
from jax.experimental.pallas import tpu as pltpu
from jax.sharding import PartitionSpec as P

KNOTS = 17
SPACING = 3.0 / (KNOTS - 1)
MESH = pl.DeviceIdType.MESH
TILE = 16
PARTS = 4
GROUPS = 2
STEPS = 8
LIFT = 2.0 ** 50


def to_wire(value):
    value = value * LIFT
    return (value * jnp.abs(value)).astype(jnp.bfloat16)


def from_wire(value):
    value = value.astype(jnp.float32)
    return value * lax.rsqrt(jnp.maximum(jnp.abs(value), 2.0 ** -126)) * (1.0 / LIFT)


def sin_cos(angle):
    n = jnp.round(angle * 0.15915494309189535)
    rest = ((angle - n * 6.28125) - n * 1.9350051879882812e-3) - n * 3.019915981956753e-7
    rest = rest * 0.25
    z = rest * rest
    sine = rest + rest * z * (-1.6666654611e-1 + z * (8.3321608736e-3 - z * 1.9515295891e-4))
    cosine = 1.0 - 0.5 * z + z * z * (
        4.166664568298827e-2 + z * (-1.388731625493765e-3 + z * 2.443315711809948e-5)
    )
    for _ in range(2):
        twice = sine + sine
        sine, cosine = twice * cosine, 1.0 - twice * sine
    return sine, cosine


def kernel(
    nb, nd, emb_ref, dir_ref, out_ref,
    raw, unit, blocks, rows_f32, waves, acc, sums, coef, grads,
    kept, pair_out, pair_in, z_own, z_out, z_in,
    raw_sem, own_sem, e_send, e_recv, f_send, s_send, s_recv, p_send, p_recv, z_send, z_recv,
):
    chips = nd // 2
    half = chips * emb_ref.shape[0]
    per = emb_ref.shape[0]
    depth = raw.shape[0]
    total_rows = half * 2 * nb
    b, d = lax.axis_index("batch"), lax.axis_index("dir")
    chip, core = d // 2, lax.rem(d, 2)
    other = 1 - core
    partner = (b, chip * 2 + other)
    step_rows = depth // STEPS

    loads = []
    for i in range(STEPS):
        part = pl.ds(i * step_rows, step_rows)
        load = pltpu.make_async_copy(dir_ref.at[part], raw.at[part], raw_sem.at[i])
        load.start()
        loads.append(load)
    own = pltpu.make_async_copy(emb_ref, blocks.at[d], own_sem)
    own.start()

    chip_peers = [lax.rem(chip + j, chips) for j in range(1, chips)]
    batch_peers = [lax.rem(b + j, nb) for j in range(1, nb)]
    barrier = pltpu.get_barrier_semaphore()
    for c in chip_peers:
        for side in (core, other):
            pl.semaphore_signal(barrier, inc=1, device_id=(b, c * 2 + side), device_id_type=MESH)
    for a in batch_peers:
        pl.semaphore_signal(barrier, inc=1, device_id=(a, d), device_id_type=MESH)
    pl.semaphore_signal(barrier, inc=1, device_id=partner, device_id_type=MESH)
    pl.semaphore_wait(barrier, 2 * len(chip_peers) + len(batch_peers) + 1)

    def send_block(src, slot, sem, device):
        return pltpu.make_async_remote_copy(
            src_ref=src, dst_ref=blocks.at[slot], send_sem=sem, recv_sem=e_recv.at[slot],
            device_id=device, device_id_type=MESH,
        )

    sent = []
    own.wait()
    for j, c in enumerate(chip_peers):
        copy = send_block(blocks.at[d], d, e_send.at[j], (b, c * 2 + core))
        copy.start()
        sent.append(copy)
    copy = send_block(blocks.at[d], d, e_send.at[chips - 1], partner)
    copy.start()
    sent.append(copy)
    for j, c in enumerate(chip_peers):
        copy = send_block(blocks.at[d], d, f_send.at[j], (b, c * 2 + other))
        copy.start()
        sent.append(copy)

    for load in loads:
        load.wait()
    width = raw.shape[1]

    def add_squares(i, square):
        part = pl.ds(pl.multiple_of(i * step_rows, step_rows), step_rows)
        value = raw[part, :].astype(jnp.float32)
        return square + jnp.sum((value * value).reshape(step_rows // 8, 8, width), axis=0)

    square = lax.fori_loop(0, STEPS, add_squares, jnp.zeros((8, width), jnp.float32))
    scale = 1.0 / jnp.sqrt(jnp.sum(square, axis=0, keepdims=True) + 1e-06)

    def normalize(i, carry):
        part = pl.ds(pl.multiple_of(i * step_rows, step_rows), step_rows)
        unit[part, :] = (raw[part, :].astype(jnp.float32) * scale).astype(jnp.bfloat16)
        return carry

    lax.fori_loop(0, STEPS, normalize, 0)

    for j, c in enumerate(chip_peers):
        slot = c * 2 + core
        send_block(emb_ref, slot, e_send.at[j], partner).wait_recv()

    wide = width // GROUPS
    knots = KNOTS - 1

    def gather_rows(which, side):
        for c in range(chips):
            rows_f32[which, c * per:(c + 1) * per, :] = blocks[c * 2 + side].astype(jnp.float32)
        return rows_f32[which].astype(jnp.bfloat16)

    def project(rows, g):
        return jnp.dot(
            rows, unit[:, g * wide:(g + 1) * wide], preferred_element_type=jnp.float32
        )

    def fold(value):
        return jnp.sum(value.reshape(TILE // 8, 8, -1), axis=0)

    def trig(which, projected, g):
        lanes = pl.ds(g * wide, wide)
        for r in range(half // TILE):
            first = which == 0 and r == 0
            at = which * half + r * TILE
            sine1, cosine1 = sin_cos(SPACING * projected[r * TILE:(r + 1) * TILE])
            powers = {1: (cosine1, sine1)}
            for k in range(1, KNOTS):
                if k > 1 and k % 2 == 0:
                    cosine, sine = powers[k // 2]
                    twice = cosine + cosine
                    powers[k] = (twice * cosine - 1.0, twice * sine)
                elif k > 1:
                    cosine, sine = powers[k - 1]
                    powers[k] = (
                        cosine * cosine1 - sine * sine1, sine * cosine1 + cosine * sine1
                    )
                for s in range(2):
                    waves[k - 1, s, at:at + TILE, lanes] = powers[k][s]
                    part = fold(powers[k][s])
                    rows = pl.ds((s * knots + k - 1) * 8, 8)
                    acc[g, rows, :] = part if first else acc[g, rows, :] + part

    home_rows = gather_rows(0, core)
    for g in range(GROUPS):
        trig(0, project(home_rows, g), g)
    send_rest = [lax.rem(chip + j, chips) * 2 + other for j in range(chips)]
    for slot in send_rest:
        send_block(emb_ref, slot, e_send.at[0], partner).wait_recv()
    away_rows = gather_rows(1, other)

    def send_sums(g, j, a, slot):
        return pltpu.make_async_remote_copy(
            src_ref=sums.at[g, b], dst_ref=sums.at[g, slot], send_sem=s_send.at[g, j],
            recv_sem=s_recv.at[g, slot], device_id=(a, d), device_id_type=MESH,
        )

    for g in range(GROUPS):
        trig(1, project(away_rows, g), g)
        value = acc[g, pl.ds(0, 2 * knots, stride=8), :]
        for i in range(1, 8):
            value = value + acc[g, pl.ds(i, 2 * knots, stride=8), :]
        sums[g, b] = value
        for j, a in enumerate(batch_peers):
            copy = send_sums(g, j, a, b)
            copy.start()
            sent.append(copy)
    knot = lax.broadcasted_iota(jnp.int32, (knots, wide), 0).astype(jnp.float32) + 1.0
    pos = knot * SPACING
    target = jnp.exp(-0.5 * pos * pos)
    ends = jnp.where(knot == float(knots), 0.5, 1.0)
    weight = 2.0 * (ends * SPACING * target)

    def coefficients(g):
        for j, a in enumerate(batch_peers):
            send_sums(g, j, a, a).wait_recv()
        total = sums[g, 0]
        for a in range(1, nb):
            total = total + sums[g, a]
        mean = total * (1.0 / total_rows)
        coef[g, 0:knots, :] = pos * (weight * (mean[0:knots] - target))
        coef[g, knots:2 * knots, :] = pos * (weight * mean[knots:2 * knots])

    ones = jnp.full((1, wide), 1.0, jnp.float32)
    zeros = jnp.zeros((1, wide), jnp.float32)
    end = 2.0 * 0.5 * SPACING
    first_term = 0.0 * (ones * (end * zeros) - zeros * (end * (ones - 1.0)))

    def grad(which, g):
        lanes = pl.ds(g * wide, wide)
        for r in range(half // TILE):
            at = which * half + r * TILE
            value = jnp.broadcast_to(first_term, (TILE, wide))
            for k in range(knots):
                value = value + (
                    waves[k, 0, at:at + TILE, lanes] * coef[g, knots + k:knots + k + 1, :]
                    - waves[k, 1, at:at + TILE, lanes] * coef[g, k:k + 1, :]
                )
            grads[at:at + TILE, lanes] = value.astype(jnp.bfloat16)

    columns = depth // PARTS

    def back(value, p):
        return lax.dot_general(
            value, unit[p * columns:(p + 1) * columns, :], (((1,), (1,)), ((), ())),
            preferred_element_type=jnp.float32,
        )

    for g in range(GROUPS):
        coefficients(g)
        for which in range(2):
            grad(which, g)
    both = grads[...]
    pairs = []
    for p in range(PARTS):
        value = back(both, p)
        kept[p] = value[0:half]
        pair_out[p] = value[half:2 * half]
        copy = pltpu.make_async_remote_copy(
            src_ref=pair_out.at[p], dst_ref=pair_in.at[p], send_sem=p_send.at[p],
            recv_sem=p_recv.at[p], device_id=partner, device_id_type=MESH,
        )
        copy.start()
        pairs.append(copy)
        sent.append(copy)
    for p in range(PARTS):
        pairs[p].wait_recv()
        value = kept[p] + pair_in[p]
        for c in range(chips):
            z_own[p, c] = value[c * per:(c + 1) * per]
            z_out[p, c] = to_wire(value[c * per:(c + 1) * per])
        for j, c in enumerate(chip_peers):
            copy = pltpu.make_async_remote_copy(
                src_ref=z_out.at[p, c], dst_ref=z_in.at[p, chip], send_sem=z_send.at[p, j],
                recv_sem=z_recv.at[p, chip], device_id=(b, c * 2 + core), device_id_type=MESH,
            )
            copy.start()
            sent.append(copy)
    for p in range(PARTS):
        value = z_own[p, chip]
        for j, c in enumerate(chip_peers):
            pltpu.make_async_remote_copy(
                src_ref=z_out.at[p, c], dst_ref=z_in.at[p, c], send_sem=z_send.at[p, j],
                recv_sem=z_recv.at[p, c], device_id=(b, c * 2 + core), device_id_type=MESH,
            ).wait_recv()
            value = value + from_wire(z_in[p, c])
        out_ref[:, p * columns:(p + 1) * columns] = value
    for copy in sent:
        copy.wait_send()


def local(nb, nd, embeddings, directions):
    per, depth = embeddings.shape
    width = directions.shape[1]
    chips = nd // 2
    half = chips * per
    knots = KNOTS - 1
    columns = depth // PARTS
    wide = width // GROUPS
    f32, bf16 = jnp.float32, jnp.bfloat16
    dma = pltpu.SemaphoreType.DMA
    return pl.pallas_call(
        functools.partial(kernel, nb, nd),
        out_shape=jax.ShapeDtypeStruct((per, depth), f32),
        in_specs=[pl.BlockSpec(memory_space=pltpu.HBM)] * 2,
        out_specs=pl.BlockSpec(memory_space=pltpu.VMEM),
        scratch_shapes=[
            pltpu.VMEM((depth, width), bf16),
            pltpu.VMEM((depth, width), bf16),
            pltpu.VMEM((nd, per, depth), bf16),
            pltpu.VMEM((2, half, depth), f32),
            pltpu.VMEM((knots, 2, 2 * half, width), f32),
            pltpu.VMEM((GROUPS, 2 * knots * 8, wide), f32),
            pltpu.VMEM((GROUPS, nb, 2 * knots, wide), f32),
            pltpu.VMEM((GROUPS, 2 * knots, wide), f32),
            pltpu.VMEM((2 * half, width), bf16),
            pltpu.VMEM((PARTS, half, columns), f32),
            pltpu.VMEM((PARTS, half, columns), f32),
            pltpu.VMEM((PARTS, half, columns), f32),
            pltpu.VMEM((PARTS, chips, per, columns), f32),
            pltpu.VMEM((PARTS, chips, per, columns), bf16),
            pltpu.VMEM((PARTS, chips, per, columns), bf16),
            dma((STEPS,)),
            dma,
            dma((chips,)),
            dma((nd,)),
            dma((chips,)),
            dma((GROUPS, nb)),
            dma((GROUPS, nb)),
            dma((PARTS,)),
            dma((PARTS,)),
            dma((PARTS, chips)),
            dma((PARTS, chips)),
        ],
        compiler_params=pltpu.CompilerParams(
            collective_id=0, has_side_effects=True, vmem_limit_bytes=56 * 1000 * 1000
        ),
        name="sigreg_backward",
    )(embeddings, directions)


def solution(mesh):
    placed = (P(("batch", "dir"), None), P(None, "dir"))
    return jax.shard_map(
        functools.partial(local, mesh.shape["batch"], mesh.shape["dir"]),
        mesh=mesh, in_specs=placed, out_specs=P(("batch", "dir"), None), check_vma=False,
    )
```

```python
import functools

import jax
import jax.numpy as jnp
from jax import lax
from jax.experimental import pallas as pl
from jax.experimental.pallas import tpu as pltpu
from jax.sharding import PartitionSpec as P

KNOTS = 17
SPACING = 3.0 / (KNOTS - 1)
MESH = pl.DeviceIdType.MESH
TILE = 16
GROUPS = 2
STEPS = 8
LIFT = 2.0 ** 50


def to_wire(value):
    value = value * LIFT
    return (value * jnp.abs(value)).astype(jnp.bfloat16)


def from_wire(value):
    value = value.astype(jnp.float32)
    return value * lax.rsqrt(jnp.maximum(jnp.abs(value), 2.0 ** -126)) * (1.0 / LIFT)


def sin_cos(angle):
    n = jnp.round(angle * 0.15915494309189535)
    rest = ((angle - n * 6.28125) - n * 1.9350051879882812e-3) - n * 3.019915981956753e-7
    rest = rest * 0.25
    z = rest * rest
    sine = rest + rest * z * (-1.6666654611e-1 + z * (8.3321608736e-3 - z * 1.9515295891e-4))
    cosine = 1.0 - 0.5 * z + z * z * (
        4.166664568298827e-2 + z * (-1.388731625493765e-3 + z * 2.443315711809948e-5)
    )
    for _ in range(2):
        twice = sine + sine
        sine, cosine = twice * cosine, 1.0 - twice * sine
    return sine, cosine


def kernel(
    nb, nd, emb_ref, dir_ref, out_ref,
    raw, unit, blocks, rows_f32, waves, acc, sums, coef, grads,
    kept, pair_out, pair_in, z_own, z_out, z_in,
    raw_sem, own_sem, e_send, e_recv, s_send, s_recv, p_send, p_recv, z_send, z_recv,
):
    chips = nd // 2
    half = chips * emb_ref.shape[0]
    per = emb_ref.shape[0]
    depth = raw.shape[0]
    total_rows = half * 2 * nb
    b, d = lax.axis_index("batch"), lax.axis_index("dir")
    chip, core = d // 2, lax.rem(d, 2)
    other = 1 - core
    partner = (b, chip * 2 + other)
    step_rows = depth // STEPS

    loads = []
    for i in range(STEPS):
        part = pl.ds(i * step_rows, step_rows)
        load = pltpu.make_async_copy(dir_ref.at[part], raw.at[part], raw_sem.at[i])
        load.start()
        loads.append(load)
    mid = depth // 2
    own = []
    for h in range(2):
        copy = pltpu.make_async_copy(
            emb_ref.at[:, pl.ds(h * mid, mid)], blocks.at[h, d], own_sem.at[h]
        )
        copy.start()
        own.append(copy)

    chip_peers = [lax.rem(chip + j, chips) for j in range(1, chips)]
    batch_peers = [lax.rem(b + j, nb) for j in range(1, nb)]
    barrier = pltpu.get_barrier_semaphore()
    for c in chip_peers:
        for side in (core, other):
            pl.semaphore_signal(barrier, inc=1, device_id=(b, c * 2 + side), device_id_type=MESH)
    for a in batch_peers:
        pl.semaphore_signal(barrier, inc=1, device_id=(a, d), device_id_type=MESH)
    pl.semaphore_signal(barrier, inc=1, device_id=partner, device_id_type=MESH)
    pl.semaphore_wait(barrier, 2 * len(chip_peers) + len(batch_peers) + 1)

    sent = []

    def send_block(h, slot, device):
        copy = pltpu.make_async_remote_copy(
            src_ref=blocks.at[h, slot], dst_ref=blocks.at[h, slot],
            send_sem=e_send.at[len(sent)], recv_sem=e_recv.at[h, slot],
            device_id=device, device_id_type=MESH,
        )
        copy.start()
        sent.append(copy)

    def take_block(h, slot):
        pltpu.make_async_remote_copy(
            src_ref=blocks.at[h, slot], dst_ref=blocks.at[h, slot],
            send_sem=e_send.at[0], recv_sem=e_recv.at[h, slot],
            device_id=partner, device_id_type=MESH,
        ).wait_recv()

    for copy in own:
        copy.wait()
    for h in range(2):
        for c in chip_peers:
            send_block(h, d, (b, c * 2 + core))
    for h in range(2):
        send_block(h, d, partner)
    for c in chip_peers:
        send_block(1, d, (b, c * 2 + other))

    for load in loads:
        load.wait()
    width = raw.shape[1]

    def add_squares(i, square):
        part = pl.ds(pl.multiple_of(i * step_rows, step_rows), step_rows)
        value = raw[part, :].astype(jnp.float32)
        return square + jnp.sum((value * value).reshape(step_rows // 8, 8, width), axis=0)

    square = lax.fori_loop(0, STEPS, add_squares, jnp.zeros((8, width), jnp.float32))
    scale = 1.0 / jnp.sqrt(jnp.sum(square, axis=0, keepdims=True) + 1e-06)

    def normalize(i, carry):
        part = pl.ds(pl.multiple_of(i * step_rows, step_rows), step_rows)
        unit[part, :] = (raw[part, :].astype(jnp.float32) * scale).astype(jnp.bfloat16)
        return carry

    lax.fori_loop(0, STEPS, normalize, 0)

    for c in chip_peers:
        take_block(0, c * 2 + core)
        send_block(0, c * 2 + core, partner)
    for c in chip_peers:
        take_block(1, c * 2 + core)

    wide = width // GROUPS
    knots = KNOTS - 1

    def gather_rows(which, side):
        for c in range(chips):
            for h in range(2):
                rows_f32[which, c * per:(c + 1) * per, h * mid:(h + 1) * mid] = blocks[
                    h, c * 2 + side
                ].astype(jnp.float32)
        return rows_f32[which].astype(jnp.bfloat16)

    def project(rows, g):
        return jnp.dot(
            rows, unit[:, g * wide:(g + 1) * wide], preferred_element_type=jnp.float32
        )

    def fold(value):
        return jnp.sum(value.reshape(TILE // 8, 8, -1), axis=0)

    def trig(which, projected, g):
        lanes = pl.ds(g * wide, wide)
        for r in range(half // TILE):
            first = which == 0 and r == 0
            at = which * half + r * TILE
            sine1, cosine1 = sin_cos(SPACING * projected[r * TILE:(r + 1) * TILE])
            powers = {1: (cosine1, sine1)}
            for k in range(1, KNOTS):
                if k > 1 and k % 2 == 0:
                    cosine, sine = powers[k // 2]
                    twice = cosine + cosine
                    powers[k] = (twice * cosine - 1.0, twice * sine)
                elif k > 1:
                    cosine, sine = powers[k - 1]
                    powers[k] = (
                        cosine * cosine1 - sine * sine1, sine * cosine1 + cosine * sine1
                    )
                for s in range(2):
                    waves[k - 1, s, at:at + TILE, lanes] = powers[k][s]
                    part = fold(powers[k][s])
                    rows = pl.ds((s * knots + k - 1) * 8, 8)
                    acc[g, rows, :] = part if first else acc[g, rows, :] + part

    home_rows = gather_rows(0, core)
    for g in range(GROUPS):
        trig(0, project(home_rows, g), g)
    for h in range(2):
        for j in range(chips):
            take_block(h, lax.rem(chip + j, chips) * 2 + other)
    away_rows = gather_rows(1, other)

    def send_sums(g, j, a, slot):
        return pltpu.make_async_remote_copy(
            src_ref=sums.at[g, b], dst_ref=sums.at[g, slot], send_sem=s_send.at[g, j],
            recv_sem=s_recv.at[g, slot], device_id=(a, d), device_id_type=MESH,
        )

    for g in range(GROUPS):
        trig(1, project(away_rows, g), g)
        value = acc[g, pl.ds(0, 2 * knots, stride=8), :]
        for i in range(1, 8):
            value = value + acc[g, pl.ds(i, 2 * knots, stride=8), :]
        sums[g, b] = value
        for j, a in enumerate(batch_peers):
            copy = send_sums(g, j, a, b)
            copy.start()
            sent.append(copy)
    knot = lax.broadcasted_iota(jnp.int32, (knots, wide), 0).astype(jnp.float32) + 1.0
    pos = knot * SPACING
    target = jnp.exp(-0.5 * pos * pos)
    ends = jnp.where(knot == float(knots), 0.5, 1.0)
    weight = 2.0 * (ends * SPACING * target)

    def coefficients(g):
        for j, a in enumerate(batch_peers):
            send_sums(g, j, a, a).wait_recv()
        total = sums[g, 0]
        for a in range(1, nb):
            total = total + sums[g, a]
        mean = total * (1.0 / total_rows)
        coef[g, 0:knots, :] = pos * (weight * (mean[0:knots] - target))
        coef[g, knots:2 * knots, :] = pos * (weight * mean[knots:2 * knots])

    ones = jnp.full((1, wide), 1.0, jnp.float32)
    zeros = jnp.zeros((1, wide), jnp.float32)
    end = 2.0 * 0.5 * SPACING
    first_term = 0.0 * (ones * (end * zeros) - zeros * (end * (ones - 1.0)))

    def grad(which, g):
        lanes = pl.ds(g * wide, wide)
        for r in range(half // TILE):
            at = which * half + r * TILE
            value = jnp.broadcast_to(first_term, (TILE, wide))
            for k in range(knots):
                value = value + (
                    waves[k, 0, at:at + TILE, lanes] * coef[g, knots + k:knots + k + 1, :]
                    - waves[k, 1, at:at + TILE, lanes] * coef[g, k:k + 1, :]
                )
            grads[at:at + TILE, lanes] = value.astype(jnp.bfloat16)

    for g in range(GROUPS):
        coefficients(g)
        for which in range(2):
            grad(which, g)
    both = grads[...]

    def back(p):
        return lax.dot_general(
            both, unit[p * mid:(p + 1) * mid, :], (((1,), (1,)), ((), ())),
            preferred_element_type=jnp.float32,
        )

    def send_sum(p, i, src, slot, device):
        return pltpu.make_async_remote_copy(
            src_ref=src, dst_ref=z_in.at[p, slot], send_sem=z_send.at[p, i],
            recv_sem=z_recv.at[p, slot], device_id=device, device_id_type=MESH,
        )

    value = back(1)
    kept[...] = value[0:half]
    pair_out[...] = value[half:2 * half]
    pair = pltpu.make_async_remote_copy(
        src_ref=pair_out, dst_ref=pair_in, send_sem=p_send, recv_sem=p_recv,
        device_id=partner, device_id_type=MESH,
    )
    pair.start()
    sent.append(pair)
    value = back(0)
    for side in range(2):
        for c in range(chips):
            rows = value[side * half + c * per:side * half + (c + 1) * per]
            if side == 0:
                z_own[0, c] = rows
            z_out[0, side, c] = to_wire(rows)
    for i, c in enumerate(chip_peers):
        for side, target in ((0, core), (1, other)):
            copy = send_sum(0, side * chips + i, z_out.at[0, side, c], d, (b, c * 2 + target))
            copy.start()
            sent.append(copy)
    copy = send_sum(0, chips - 1, z_out.at[0, 1, chip], d, partner)
    copy.start()
    sent.append(copy)
    pair.wait_recv()
    value = kept[...] + pair_in[...]
    for c in range(chips):
        rows = value[c * per:(c + 1) * per]
        z_own[1, c] = rows
        z_out[1, 0, c] = to_wire(rows)
    for i, c in enumerate(chip_peers):
        copy = send_sum(1, i, z_out.at[1, 0, c], d, (b, c * 2 + core))
        copy.start()
        sent.append(copy)

    def take_sum(p, slot):
        send_sum(p, 0, z_out.at[0, 0, 0], slot, partner).wait_recv()
        return from_wire(z_in[p, slot])

    value = z_own[0, chip] + take_sum(0, chip * 2 + other)
    for c in chip_peers:
        for side in (core, other):
            value = value + take_sum(0, c * 2 + side)
    out_ref[:, 0:mid] = value
    value = z_own[1, chip]
    for c in chip_peers:
        value = value + take_sum(1, c * 2 + core)
    out_ref[:, mid:depth] = value
    for copy in sent:
        copy.wait_send()


def local(nb, nd, embeddings, directions):
    per, depth = embeddings.shape
    width = directions.shape[1]
    chips = nd // 2
    half = chips * per
    knots = KNOTS - 1
    mid = depth // 2
    wide = width // GROUPS
    f32, bf16 = jnp.float32, jnp.bfloat16
    dma = pltpu.SemaphoreType.DMA
    return pl.pallas_call(
        functools.partial(kernel, nb, nd),
        out_shape=jax.ShapeDtypeStruct((per, depth), f32),
        in_specs=[pl.BlockSpec(memory_space=pltpu.HBM)] * 2,
        out_specs=pl.BlockSpec(memory_space=pltpu.VMEM),
        scratch_shapes=[
            pltpu.VMEM((depth, width), bf16),
            pltpu.VMEM((depth, width), bf16),
            pltpu.VMEM((2, nd, per, mid), bf16),
            pltpu.VMEM((2, half, depth), f32),
            pltpu.VMEM((knots, 2, 2 * half, width), f32),
            pltpu.VMEM((GROUPS, 2 * knots * 8, wide), f32),
            pltpu.VMEM((GROUPS, nb, 2 * knots, wide), f32),
            pltpu.VMEM((GROUPS, 2 * knots, wide), f32),
            pltpu.VMEM((2 * half, width), bf16),
            pltpu.VMEM((half, mid), f32),
            pltpu.VMEM((half, mid), f32),
            pltpu.VMEM((half, mid), f32),
            pltpu.VMEM((2, chips, per, mid), f32),
            pltpu.VMEM((2, 2, chips, per, mid), bf16),
            pltpu.VMEM((2, nd, per, mid), bf16),
            dma((STEPS,)),
            dma((2,)),
            dma((4 * chips,)),
            dma((2, nd)),
            dma((GROUPS, nb)),
            dma((GROUPS, nb)),
            dma,
            dma,
            dma((2, nd)),
            dma((2, nd)),
        ],
        compiler_params=pltpu.CompilerParams(
            collective_id=0, has_side_effects=True, vmem_limit_bytes=56 * 1000 * 1000
        ),
        name="sigreg_backward",
    )(embeddings, directions)


def solution(mesh):
    placed = (P(("batch", "dir"), None), P(None, "dir"))
    return jax.shard_map(
        functools.partial(local, mesh.shape["batch"], mesh.shape["dir"]),
        mesh=mesh, in_specs=placed, out_specs=P(("batch", "dir"), None), check_vma=False,
    )
```

```python
import functools

import jax
import jax.numpy as jnp
from jax import lax
from jax.experimental import pallas as pl
from jax.experimental.pallas import tpu as pltpu
from jax.sharding import PartitionSpec as P

KNOTS = 17
SPACING = 3.0 / (KNOTS - 1)
MESH = pl.DeviceIdType.MESH
TILE = 16
PARTS = 2
STEPS = 8
LIFT = 2.0 ** 50


def to_wire(value):
    value = value * LIFT
    return (value * jnp.abs(value)).astype(jnp.bfloat16)


def from_wire(value):
    value = value.astype(jnp.float32)
    return value * lax.rsqrt(jnp.maximum(jnp.abs(value), 2.0 ** -126)) * (1.0 / LIFT)


def sin_cos(angle):
    n = jnp.round(angle * 0.15915494309189535)
    rest = ((angle - n * 6.28125) - n * 1.9350051879882812e-3) - n * 3.019915981956753e-7
    rest = rest * 0.25
    z = rest * rest
    sine = rest + rest * z * (-1.6666654611e-1 + z * (8.3321608736e-3 - z * 1.9515295891e-4))
    cosine = 1.0 - 0.5 * z + z * z * (
        4.166664568298827e-2 + z * (-1.388731625493765e-3 + z * 2.443315711809948e-5)
    )
    for _ in range(2):
        twice = sine + sine
        sine, cosine = twice * cosine, 1.0 - twice * sine
    return sine, cosine


def kernel(
    nb, nd, emb_ref, dir_ref, out_ref,
    raw, unit, blocks, rows_f32, waves, acc, sums, coef, grads,
    kept, pair_out, pair_in, z_own, z_out, z_in,
    raw_sem, own_sem, e_send, e_recv, f_send, f_recv, s_send, s_recv, p_send, p_recv, z_send, z_recv,
):
    chips = nd // 2
    half = chips * emb_ref.shape[0]
    per = emb_ref.shape[0]
    depth = raw.shape[0]
    total_rows = half * 2 * nb
    b, d = lax.axis_index("batch"), lax.axis_index("dir")
    chip, core = d // 2, lax.rem(d, 2)
    other = 1 - core
    partner = (b, chip * 2 + other)
    step_rows = depth // STEPS

    def remote(src, dst, send_sem, recv_sem, device):
        return pltpu.make_async_remote_copy(
            src_ref=src, dst_ref=dst, send_sem=send_sem, recv_sem=recv_sem,
            device_id=device, device_id_type=MESH,
        )

    def wait_all(ref, sem):
        pltpu.make_async_copy(ref, ref, sem).wait()

    load = pltpu.make_async_copy(dir_ref, raw, raw_sem)
    load.start()
    own = pltpu.make_async_copy(emb_ref, blocks.at[core, chip], own_sem)
    own.start()

    chip_peers = [lax.rem(chip + j, chips) for j in range(1, chips)]
    batch_peers = [lax.rem(b + j, nb) for j in range(1, nb)]
    barrier = pltpu.get_barrier_semaphore()
    for c in chip_peers:
        pl.semaphore_signal(barrier, inc=1, device_id=(b, c * 2 + core), device_id_type=MESH)
    for a in batch_peers:
        pl.semaphore_signal(barrier, inc=1, device_id=(a, d), device_id_type=MESH)
    pl.semaphore_signal(barrier, inc=1, device_id=partner, device_id_type=MESH)
    pl.semaphore_wait(barrier, len(chip_peers) + len(batch_peers) + 1)

    mine = blocks.at[core, chip]
    own.wait()
    for c in chip_peers:
        remote(mine, mine, e_send, e_recv.at[chip], (b, c * 2 + core)).start()
    remote(mine, mine, e_send, f_recv, partner).start()

    load.wait()
    width = raw.shape[1]

    def add_squares(i, square):
        part = pl.ds(pl.multiple_of(i * step_rows, step_rows), step_rows)
        value = raw[part, :].astype(jnp.float32)
        return square + jnp.sum((value * value).reshape(step_rows // 8, 8, width), axis=0)

    square = lax.fori_loop(0, STEPS, add_squares, jnp.zeros((8, width), jnp.float32))
    scale = 1.0 / jnp.sqrt(jnp.sum(square, axis=0, keepdims=True) + 1e-06)

    def normalize(i, carry):
        part = pl.ds(pl.multiple_of(i * step_rows, step_rows), step_rows)
        unit[part, :] = (raw[part, :].astype(jnp.float32) * scale).astype(jnp.bfloat16)
        return carry

    lax.fori_loop(0, STEPS, normalize, 0)

    for c in chip_peers:
        block = blocks.at[core, c]
        remote(block, block, f_send, e_recv.at[c], partner).wait_recv()
        remote(block, block, f_send, f_recv, partner).start()

    knots = KNOTS - 1

    def project(which, side):
        for c in range(chips):
            rows_f32[c * per:(c + 1) * per, :] = blocks[side, c].astype(jnp.float32)
        return jnp.dot(
            rows_f32[...].astype(jnp.bfloat16), unit[...], preferred_element_type=jnp.float32
        )

    def fold(value):
        return jnp.sum(value.reshape(TILE // 8, 8, -1), axis=0)

    def trig(which, projected):
        for r in range(half // TILE):
            first = which == 0 and r == 0
            at = which * half + r * TILE
            sine1, cosine1 = sin_cos(SPACING * projected[r * TILE:(r + 1) * TILE])
            powers = {1: (cosine1, sine1)}
            for k in range(1, KNOTS):
                if k > 1 and k % 2 == 0:
                    cosine, sine = powers[k // 2]
                    twice = cosine + cosine
                    powers[k] = (twice * cosine - 1.0, twice * sine)
                elif k > 1:
                    (cos_a, sin_a), (cos_b, sin_b) = powers[k // 2], powers[k // 2 + 1]
                    powers[k] = (cos_a * cos_b - sin_a * sin_b, sin_a * cos_b + cos_a * sin_b)
                for s in range(2):
                    waves[k - 1, s, at:at + TILE, :] = powers[k][s]
                    part = fold(powers[k][s])
                    rows = pl.ds((s * knots + k - 1) * 8, 8)
                    for v in range(width // 128):
                        piece = part[:, v * 128:(v + 1) * 128]
                        acc[v, rows, :] = piece if first else acc[v, rows, :] + piece

    trig(0, project(0, core))
    wait_all(blocks.at[other], f_recv)
    trig(1, project(1, other))
    for v in range(width // 128):
        value = acc[v, pl.ds(0, 2 * knots, stride=8), :]
        for i in range(1, 8):
            value = value + acc[v, pl.ds(i, 2 * knots, stride=8), :]
        sums[b, :, v * 128:(v + 1) * 128] = value
    for a in batch_peers:
        remote(sums.at[b], sums.at[b], s_send, s_recv, (a, d)).start()

    knot = lax.broadcasted_iota(jnp.int32, (knots, width), 0).astype(jnp.float32) + 1.0
    pos = knot * SPACING
    target = jnp.exp(-0.5 * pos * pos)
    ends = jnp.where(knot == float(knots), 0.5, 1.0)
    weight = 2.0 * (ends * SPACING * target)
    wait_all(blocks.at[0], e_send)
    if chips > 1:
        wait_all(blocks.at[0, pl.ds(0, chips - 1)], f_send)
    if nb > 1:
        wait_all(sums.at[pl.ds(0, nb - 1)], s_recv)
    total = sums[0]
    for a in range(1, nb):
        total = total + sums[a]
    mean = total * (1.0 / total_rows)
    coef[0:knots, :] = pos * (weight * (mean[0:knots] - target))
    coef[knots:2 * knots, :] = pos * (weight * mean[knots:2 * knots])
    ones = jnp.full((1, width), 1.0, jnp.float32)
    zeros = jnp.zeros((1, width), jnp.float32)
    end = 2.0 * 0.5 * SPACING
    first_term = 0.0 * (ones * (end * zeros) - zeros * (end * (ones - 1.0)))

    for at in range(0, 2 * half, TILE):
        value = jnp.broadcast_to(first_term, (TILE, width))
        for k in range(knots):
            value = value + (
                waves[k, 0, at:at + TILE, :] * coef[knots + k:knots + k + 1, :]
                - waves[k, 1, at:at + TILE, :] * coef[k:k + 1, :]
            )
        grads[at:at + TILE, :] = value.astype(jnp.bfloat16)

    columns = depth // PARTS

    def back(value, p):
        return lax.dot_general(
            value, unit[p * columns:(p + 1) * columns, :], (((1,), (1,)), ((), ())),
            preferred_element_type=jnp.float32,
        )

    both = grads[...]
    for p in range(PARTS):
        value = back(both, p)
        kept[p] = value[0:half]
        pair_out[p] = value[half:2 * half]
        remote(pair_out.at[p], pair_in.at[p], p_send, p_recv.at[p], partner).start()
    for p in range(PARTS):
        wait_all(pair_in.at[p], p_recv.at[p])
        value = kept[p] + pair_in[p]
        for c in range(chips):
            z_own[p, c] = value[c * per:(c + 1) * per]
            z_out[p, c] = to_wire(value[c * per:(c + 1) * per])
        for c in chip_peers:
            remote(
                z_out.at[p, c], z_in.at[p, chip], z_send, z_recv.at[p], (b, c * 2 + core)
            ).start()
    if nb > 1:
        wait_all(sums.at[pl.ds(0, nb - 1)], s_send)
    wait_all(pair_out, p_send)
    for p in range(PARTS):
        value = z_own[p, chip]
        if chips > 1:
            wait_all(z_in.at[p, pl.ds(0, chips - 1)], z_recv.at[p])
        for c in chip_peers:
            value = value + from_wire(z_in[p, c])
        out_ref[:, p * columns:(p + 1) * columns] = value
    if chips > 1:
        wait_all(z_out.at[:, pl.ds(0, chips - 1)], z_send)


def local(nb, nd, embeddings, directions):
    per, depth = embeddings.shape
    width = directions.shape[1]
    chips = nd // 2
    half = chips * per
    knots = KNOTS - 1
    columns = depth // PARTS
    f32, bf16 = jnp.float32, jnp.bfloat16
    dma = pltpu.SemaphoreType.DMA
    return pl.pallas_call(
        functools.partial(kernel, nb, nd),
        out_shape=jax.ShapeDtypeStruct((per, depth), f32),
        in_specs=[pl.BlockSpec(memory_space=pltpu.HBM)] * 2,
        out_specs=pl.BlockSpec(memory_space=pltpu.VMEM),
        scratch_shapes=[
            pltpu.VMEM((depth, width), bf16),
            pltpu.VMEM((depth, width), bf16),
            pltpu.VMEM((2, chips, per, depth), bf16),
            pltpu.VMEM((half, depth), f32),
            pltpu.VMEM((knots, 2, 2 * half, width), f32),
            pltpu.VMEM((width // 128, 2 * knots * 8, 128), f32),
            pltpu.VMEM((nb, 2 * knots, width), f32),
            pltpu.VMEM((2 * knots, width), f32),
            pltpu.VMEM((2 * half, width), bf16),
            pltpu.VMEM((PARTS, half, columns), f32),
            pltpu.VMEM((PARTS, half, columns), f32),
            pltpu.VMEM((PARTS, half, columns), f32),
            pltpu.VMEM((PARTS, chips, per, columns), f32),
            pltpu.VMEM((PARTS, chips, per, columns), bf16),
            pltpu.VMEM((PARTS, chips, per, columns), bf16),
            dma,
            dma,
            dma,
            dma((chips,)),
            dma,
            dma,
            dma,
            dma,
            dma,
            dma((PARTS,)),
            dma,
            dma((PARTS,)),
        ],
        compiler_params=pltpu.CompilerParams(
            collective_id=0, has_side_effects=True, vmem_limit_bytes=56 * 1000 * 1000
        ),
        name="sigreg_backward",
    )(embeddings, directions)


def solution(mesh):
    placed = (P(("batch", "dir"), None), P(None, "dir"))
    return jax.shard_map(
        functools.partial(local, mesh.shape["batch"], mesh.shape["dir"]),
        mesh=mesh, in_specs=placed, out_specs=P(("batch", "dir"), None), check_vma=False,
    )
```

```python
import functools

import jax
import jax.numpy as jnp
from jax import lax
from jax.experimental import pallas as pl
from jax.experimental.pallas import tpu as pltpu
from jax.sharding import PartitionSpec as P

KNOTS = 17
SPACING = 3.0 / (KNOTS - 1)
MESH = pl.DeviceIdType.MESH
TILE = 16
PARTS = 2
STEPS = 8
LIFT = 2.0 ** 50


def to_wire(value):
    value = value * LIFT
    return (value * jnp.abs(value)).astype(jnp.bfloat16)


def from_wire(value):
    value = value.astype(jnp.float32)
    return value * lax.rsqrt(jnp.maximum(jnp.abs(value), 2.0 ** -126)) * (1.0 / LIFT)


def sin_cos(angle):
    n = jnp.round(angle * 0.15915494309189535)
    rest = ((angle - n * 6.28125) - n * 1.9350051879882812e-3) - n * 3.019915981956753e-7
    rest = rest * 0.25
    z = rest * rest
    sine = rest + rest * z * (-1.6666654611e-1 + z * (8.3321608736e-3 - z * 1.9515295891e-4))
    cosine = 1.0 - 0.5 * z + z * z * (
        4.166664568298827e-2 + z * (-1.388731625493765e-3 + z * 2.443315711809948e-5)
    )
    for _ in range(2):
        twice = sine + sine
        sine, cosine = twice * cosine, 1.0 - twice * sine
    return sine, cosine


def kernel(
    nb, nd, emb_ref, dir_ref, out_ref,
    raw, unit, blocks, rows_f32, waves, acc, sums, coef, grads,
    kept, pair_out, pair_in, z_own, z_out, z_in,
    raw_sem, own_sem, up_send, down_send, e_recv, f_send, f_recv, s_send, s_recv, p_send, p_recv, z_send, z_recv,
):
    chips = nd // 2
    half = chips * emb_ref.shape[0]
    per = emb_ref.shape[0]
    depth = raw.shape[0]
    total_rows = half * 2 * nb
    b, d = lax.axis_index("batch"), lax.axis_index("dir")
    chip, core = d // 2, lax.rem(d, 2)
    other = 1 - core
    partner = (b, chip * 2 + other)
    step_rows = depth // STEPS

    def remote(src, dst, send_sem, recv_sem, device):
        return pltpu.make_async_remote_copy(
            src_ref=src, dst_ref=dst, send_sem=send_sem, recv_sem=recv_sem,
            device_id=device, device_id_type=MESH,
        )

    def wait_all(ref, sem):
        pltpu.make_async_copy(ref, ref, sem).wait()

    load = pltpu.make_async_copy(dir_ref, raw, raw_sem)
    load.start()
    own = pltpu.make_async_copy(emb_ref, blocks.at[core, chip], own_sem)
    own.start()

    chip_peers = [lax.rem(chip + j, chips) for j in range(1, chips)]
    batch_peers = [lax.rem(b + j, nb) for j in range(1, nb)]
    barrier = pltpu.get_barrier_semaphore()
    has_low, has_high = chip > 0, chip < chips - 1
    low, high = (b, d - 2), (b, d + 2)

    @pl.when(has_low)
    def _():
        pl.semaphore_signal(barrier, inc=1, device_id=low, device_id_type=MESH)

    @pl.when(has_high)
    def _():
        pl.semaphore_signal(barrier, inc=1, device_id=high, device_id_type=MESH)

    pl.semaphore_signal(barrier, inc=1, device_id=partner, device_id_type=MESH)
    for a in batch_peers:
        pl.semaphore_signal(barrier, inc=1, device_id=(a, d), device_id_type=MESH)
    own.wait()
    neighbors = (chip + chips - 1) // chips + (2 * chips - 2 - chip) // chips
    pl.semaphore_wait(barrier, len(batch_peers) + 1 + neighbors)

    def go_up(c):
        block = blocks.at[core, c]
        return remote(block, block, up_send.at[c], e_recv.at[c], high)

    def go_down(c):
        block = blocks.at[core, c]
        return remote(block, block, down_send.at[c], e_recv.at[c], low)

    def go_across(c):
        block = blocks.at[core, c]
        return remote(block, block, f_send, f_recv, partner)

    @pl.when(has_high)
    def _():
        go_up(chip).start()

    @pl.when(has_low)
    def _():
        go_down(chip).start()

    go_across(chip).start()

    load.wait()
    width = raw.shape[1]

    def add_squares(i, square):
        part = pl.ds(pl.multiple_of(i * step_rows, step_rows), step_rows)
        value = raw[part, :].astype(jnp.float32)
        return square + jnp.sum((value * value).reshape(step_rows // 8, 8, width), axis=0)

    square = lax.fori_loop(0, STEPS, add_squares, jnp.zeros((8, width), jnp.float32))
    scale = 1.0 / jnp.sqrt(jnp.sum(square, axis=0, keepdims=True) + 1e-06)

    def relay(step):
        below, above = chip - step, chip + step

        @pl.when(below >= 0)
        def _():
            go_up(below).wait_recv()

            @pl.when(has_high)
            def _():
                go_up(below).start()

            go_across(below).start()

        @pl.when(above < chips)
        def _():
            go_down(above).wait_recv()

            @pl.when(has_low)
            def _():
                go_down(above).start()

            go_across(above).start()

    if chips > 1:
        relay(1)

    def normalize(i, carry):
        part = pl.ds(pl.multiple_of(i * step_rows, step_rows), step_rows)
        unit[part, :] = (raw[part, :].astype(jnp.float32) * scale).astype(jnp.bfloat16)
        return carry

    lax.fori_loop(0, STEPS, normalize, 0)

    for step in range(2, chips):
        relay(step)

    knots = KNOTS - 1

    def project(which, side):
        for c in range(chips):
            rows_f32[c * per:(c + 1) * per, :] = blocks[side, c].astype(jnp.float32)
        return jnp.dot(
            rows_f32[...].astype(jnp.bfloat16), unit[...], preferred_element_type=jnp.float32
        )

    def fold(value):
        return jnp.sum(value.reshape(TILE // 8, 8, -1), axis=0)

    def trig(which, projected):
        for r in range(half // TILE):
            first = which == 0 and r == 0
            at = which * half + r * TILE
            sine1, cosine1 = sin_cos(SPACING * projected[r * TILE:(r + 1) * TILE])
            powers = {1: (cosine1, sine1)}
            for k in range(1, KNOTS):
                if k > 1 and k % 2 == 0:
                    cosine, sine = powers[k // 2]
                    twice = cosine + cosine
                    powers[k] = (twice * cosine - 1.0, twice * sine)
                elif k > 1:
                    (cos_a, sin_a), (cos_b, sin_b) = powers[k // 2], powers[k // 2 + 1]
                    powers[k] = (cos_a * cos_b - sin_a * sin_b, sin_a * cos_b + cos_a * sin_b)
                for s in range(2):
                    waves[k - 1, s, at:at + TILE, :] = powers[k][s]
                    part = fold(powers[k][s])
                    rows = pl.ds((s * knots + k - 1) * 8, 8)
                    for v in range(width // 128):
                        piece = part[:, v * 128:(v + 1) * 128]
                        acc[v, rows, :] = piece if first else acc[v, rows, :] + piece

    trig(0, project(0, core))
    wait_all(blocks.at[other], f_recv)
    trig(1, project(1, other))
    for v in range(width // 128):
        value = acc[v, pl.ds(0, 2 * knots, stride=8), :]
        for i in range(1, 8):
            value = value + acc[v, pl.ds(i, 2 * knots, stride=8), :]
        sums[b, :, v * 128:(v + 1) * 128] = value
    for a in batch_peers:
        remote(sums.at[b], sums.at[b], s_send, s_recv, (a, d)).start()

    knot = lax.broadcasted_iota(jnp.int32, (knots, width), 0).astype(jnp.float32) + 1.0
    pos = knot * SPACING
    target = jnp.exp(-0.5 * pos * pos)
    ends = jnp.where(knot == float(knots), 0.5, 1.0)
    weight = 2.0 * (ends * SPACING * target)
    for step in range(chips):
        below, above = chip - step, chip + step

        @pl.when((below >= 0) & has_high)
        def _():
            go_up(below).wait_send()

        @pl.when((above < chips) & has_low)
        def _():
            go_down(above).wait_send()

    wait_all(blocks.at[0], f_send)
    if nb > 1:
        wait_all(sums.at[pl.ds(0, nb - 1)], s_recv)
    total = sums[0]
    for a in range(1, nb):
        total = total + sums[a]
    mean = total * (1.0 / total_rows)
    coef[0:knots, :] = pos * (weight * (mean[0:knots] - target))
    coef[knots:2 * knots, :] = pos * (weight * mean[knots:2 * knots])
    ones = jnp.full((1, width), 1.0, jnp.float32)
    zeros = jnp.zeros((1, width), jnp.float32)
    end = 2.0 * 0.5 * SPACING
    first_term = 0.0 * (ones * (end * zeros) - zeros * (end * (ones - 1.0)))

    for at in range(0, 2 * half, TILE):
        value = jnp.broadcast_to(first_term, (TILE, width))
        for k in range(knots):
            value = value + (
                waves[k, 0, at:at + TILE, :] * coef[knots + k:knots + k + 1, :]
                - waves[k, 1, at:at + TILE, :] * coef[k:k + 1, :]
            )
        grads[at:at + TILE, :] = value.astype(jnp.bfloat16)

    columns = depth // PARTS

    def back(value, p):
        return lax.dot_general(
            value, unit[p * columns:(p + 1) * columns, :], (((1,), (1,)), ((), ())),
            preferred_element_type=jnp.float32,
        )

    both = grads[...]
    for p in range(PARTS):
        value = back(both, p)
        kept[p] = value[0:half]
        pair_out[p] = value[half:2 * half]
        remote(pair_out.at[p], pair_in.at[p], p_send, p_recv.at[p], partner).start()
    for p in range(PARTS):
        wait_all(pair_in.at[p], p_recv.at[p])
        value = kept[p] + pair_in[p]
        for c in range(chips):
            z_own[p, c] = value[c * per:(c + 1) * per]
            z_out[p, c] = to_wire(value[c * per:(c + 1) * per])
        for c in chip_peers:
            remote(
                z_out.at[p, c], z_in.at[p, chip], z_send, z_recv.at[p], (b, c * 2 + core)
            ).start()
    if nb > 1:
        wait_all(sums.at[pl.ds(0, nb - 1)], s_send)
    wait_all(pair_out, p_send)
    for p in range(PARTS):
        value = z_own[p, chip]
        if chips > 1:
            wait_all(z_in.at[p, pl.ds(0, chips - 1)], z_recv.at[p])
        for c in chip_peers:
            value = value + from_wire(z_in[p, c])
        out_ref[:, p * columns:(p + 1) * columns] = value
    if chips > 1:
        wait_all(z_out.at[:, pl.ds(0, chips - 1)], z_send)


def local(nb, nd, embeddings, directions):
    per, depth = embeddings.shape
    width = directions.shape[1]
    chips = nd // 2
    half = chips * per
    knots = KNOTS - 1
    columns = depth // PARTS
    f32, bf16 = jnp.float32, jnp.bfloat16
    dma = pltpu.SemaphoreType.DMA
    return pl.pallas_call(
        functools.partial(kernel, nb, nd),
        out_shape=jax.ShapeDtypeStruct((per, depth), f32),
        in_specs=[pl.BlockSpec(memory_space=pltpu.HBM)] * 2,
        out_specs=pl.BlockSpec(memory_space=pltpu.VMEM),
        scratch_shapes=[
            pltpu.VMEM((depth, width), bf16),
            pltpu.VMEM((depth, width), bf16),
            pltpu.VMEM((2, chips, per, depth), bf16),
            pltpu.VMEM((half, depth), f32),
            pltpu.VMEM((knots, 2, 2 * half, width), f32),
            pltpu.VMEM((width // 128, 2 * knots * 8, 128), f32),
            pltpu.VMEM((nb, 2 * knots, width), f32),
            pltpu.VMEM((2 * knots, width), f32),
            pltpu.VMEM((2 * half, width), bf16),
            pltpu.VMEM((PARTS, half, columns), f32),
            pltpu.VMEM((PARTS, half, columns), f32),
            pltpu.VMEM((PARTS, half, columns), f32),
            pltpu.VMEM((PARTS, chips, per, columns), f32),
            pltpu.VMEM((PARTS, chips, per, columns), bf16),
            pltpu.VMEM((PARTS, chips, per, columns), bf16),
            dma,
            dma,
            dma((chips,)),
            dma((chips,)),
            dma((chips,)),
            dma,
            dma,
            dma,
            dma,
            dma,
            dma((PARTS,)),
            dma,
            dma((PARTS,)),
        ],
        compiler_params=pltpu.CompilerParams(
            collective_id=0, has_side_effects=True, vmem_limit_bytes=56 * 1000 * 1000
        ),
        name="sigreg_backward",
    )(embeddings, directions)


def solution(mesh):
    placed = (P(("batch", "dir"), None), P(None, "dir"))
    return jax.shard_map(
        functools.partial(local, mesh.shape["batch"], mesh.shape["dir"]),
        mesh=mesh, in_specs=placed, out_specs=P(("batch", "dir"), None), check_vma=False,
    )
```

```python
import functools

import jax
import jax.numpy as jnp
from jax import lax
from jax.experimental import pallas as pl
from jax.experimental.pallas import tpu as pltpu
from jax.sharding import PartitionSpec as P

KNOTS = 17
SPACING = 3.0 / (KNOTS - 1)
MESH = pl.DeviceIdType.MESH
TILE = 16
PARTS = 2
STEPS = 8
LIFT = 2.0 ** 50


def to_wire(value):
    value = value * LIFT
    return (value * jnp.abs(value)).astype(jnp.bfloat16)


def from_wire(value):
    value = value.astype(jnp.float32)
    return value * lax.rsqrt(jnp.maximum(jnp.abs(value), 2.0 ** -126)) * (1.0 / LIFT)


def sin_cos(angle):
    n = jnp.round(angle * 0.15915494309189535)
    rest = ((angle - n * 6.28125) - n * 1.9350051879882812e-3) - n * 3.019915981956753e-7
    rest = rest * 0.25
    z = rest * rest
    sine = rest + rest * z * (-1.6666654611e-1 + z * (8.3321608736e-3 - z * 1.9515295891e-4))
    cosine = 1.0 - 0.5 * z + z * z * (
        4.166664568298827e-2 + z * (-1.388731625493765e-3 + z * 2.443315711809948e-5)
    )
    for _ in range(2):
        twice = sine + sine
        sine, cosine = twice * cosine, 1.0 - twice * sine
    return sine, cosine


def kernel(
    nb, nd, emb_ref, dir_ref, out_ref,
    raw, unit, blocks, rows_f32, waves, acc, sums, coef, grads,
    kept, pair_out, pair_in, z_own, z_out, z_in,
    raw_sem, own_sem, e_send, e_recv, f_send, f_recv, s_send, s_recv, p_send, p_recv, z_send, z_recv,
):
    chips = nd // 2
    half = chips * emb_ref.shape[0]
    per = emb_ref.shape[0]
    depth = raw.shape[0]
    total_rows = half * 2 * nb
    b, d = lax.axis_index("batch"), lax.axis_index("dir")
    chip, core = d // 2, lax.rem(d, 2)
    other = 1 - core
    partner = (b, chip * 2 + other)
    step_rows = depth // STEPS

    def remote(src, dst, send_sem, recv_sem, device):
        return pltpu.make_async_remote_copy(
            src_ref=src, dst_ref=dst, send_sem=send_sem, recv_sem=recv_sem,
            device_id=device, device_id_type=MESH,
        )

    def wait_all(ref, sem):
        pltpu.make_async_copy(ref, ref, sem).wait()

    load = pltpu.make_async_copy(dir_ref, raw, raw_sem)
    load.start()
    own = pltpu.make_async_copy(emb_ref, blocks.at[core, chip], own_sem)
    own.start()

    upper = (2 * chip) // chips
    near_end = upper * chip + (1 - upper) * (chips - 1 - chip)
    chip_peers = []
    for j in range(chips - 1):
        c = j + (j + chips - near_end) // chips
        chip_peers.append(upper * c + (1 - upper) * (chips - 1 - c))
    batch_peers = [lax.rem(b + j, nb) for j in range(1, nb)]
    barrier = pltpu.get_barrier_semaphore()
    for c in chip_peers:
        pl.semaphore_signal(barrier, inc=1, device_id=(b, c * 2 + core), device_id_type=MESH)
    for a in batch_peers:
        pl.semaphore_signal(barrier, inc=1, device_id=(a, d), device_id_type=MESH)
    pl.semaphore_signal(barrier, inc=1, device_id=partner, device_id_type=MESH)
    pl.semaphore_wait(barrier, len(chip_peers) + len(batch_peers) + 1)

    mine = blocks.at[core, chip]
    own.wait()
    for c in chip_peers:
        remote(mine, mine, e_send, e_recv.at[chip], (b, c * 2 + core)).start()
    remote(mine, mine, e_send, f_recv, partner).start()

    load.wait()
    width = raw.shape[1]

    def add_squares(i, square):
        part = pl.ds(pl.multiple_of(i * step_rows, step_rows), step_rows)
        value = raw[part, :].astype(jnp.float32)
        return square + jnp.sum((value * value).reshape(step_rows // 8, 8, width), axis=0)

    square = lax.fori_loop(0, STEPS, add_squares, jnp.zeros((8, width), jnp.float32))
    scale = 1.0 / jnp.sqrt(jnp.sum(square, axis=0, keepdims=True) + 1e-06)

    def normalize(i, carry):
        part = pl.ds(pl.multiple_of(i * step_rows, step_rows), step_rows)
        unit[part, :] = (raw[part, :].astype(jnp.float32) * scale).astype(jnp.bfloat16)
        return carry

    lax.fori_loop(0, STEPS, normalize, 0)

    for c in reversed(chip_peers):
        block = blocks.at[core, c]
        remote(block, block, f_send, e_recv.at[c], partner).wait_recv()
        remote(block, block, f_send, f_recv, partner).start()

    knots = KNOTS - 1

    def project(which, side):
        for c in range(chips):
            rows_f32[c * per:(c + 1) * per, :] = blocks[side, c].astype(jnp.float32)
        return jnp.dot(
            rows_f32[...].astype(jnp.bfloat16), unit[...], preferred_element_type=jnp.float32
        )

    def fold(value):
        return jnp.sum(value.reshape(TILE // 8, 8, -1), axis=0)

    def trig(which, projected):
        for r in range(half // TILE):
            first = which == 0 and r == 0
            at = which * half + r * TILE
            sine1, cosine1 = sin_cos(SPACING * projected[r * TILE:(r + 1) * TILE])
            powers = {1: (cosine1, sine1)}
            for k in range(1, KNOTS):
                if k > 1 and k % 2 == 0:
                    cosine, sine = powers[k // 2]
                    twice = cosine + cosine
                    powers[k] = (twice * cosine - 1.0, twice * sine)
                elif k > 1:
                    (cos_a, sin_a), (cos_b, sin_b) = powers[k // 2], powers[k // 2 + 1]
                    powers[k] = (cos_a * cos_b - sin_a * sin_b, sin_a * cos_b + cos_a * sin_b)
                for s in range(2):
                    waves[k - 1, s, at:at + TILE, :] = powers[k][s]
                    part = fold(powers[k][s])
                    rows = pl.ds((s * knots + k - 1) * 8, 8)
                    for v in range(width // 128):
                        piece = part[:, v * 128:(v + 1) * 128]
                        acc[v, rows, :] = piece if first else acc[v, rows, :] + piece

    trig(0, project(0, core))
    wait_all(blocks.at[other], f_recv)
    trig(1, project(1, other))
    for v in range(width // 128):
        value = acc[v, pl.ds(0, 2 * knots, stride=8), :]
        for i in range(1, 8):
            value = value + acc[v, pl.ds(i, 2 * knots, stride=8), :]
        sums[b, :, v * 128:(v + 1) * 128] = value
    for a in batch_peers:
        remote(sums.at[b], sums.at[b], s_send, s_recv, (a, d)).start()

    knot = lax.broadcasted_iota(jnp.int32, (knots, width), 0).astype(jnp.float32) + 1.0
    pos = knot * SPACING
    target = jnp.exp(-0.5 * pos * pos)
    ends = jnp.where(knot == float(knots), 0.5, 1.0)
    weight = 2.0 * (ends * SPACING * target)
    wait_all(blocks.at[0], e_send)
    if chips > 1:
        wait_all(blocks.at[0, pl.ds(0, chips - 1)], f_send)
    if nb > 1:
        wait_all(sums.at[pl.ds(0, nb - 1)], s_recv)
    total = sums[0]
    for a in range(1, nb):
        total = total + sums[a]
    mean = total * (1.0 / total_rows)
    coef[0:knots, :] = pos * (weight * (mean[0:knots] - target))
    coef[knots:2 * knots, :] = pos * (weight * mean[knots:2 * knots])
    ones = jnp.full((1, width), 1.0, jnp.float32)
    zeros = jnp.zeros((1, width), jnp.float32)
    end = 2.0 * 0.5 * SPACING
    first_term = 0.0 * (ones * (end * zeros) - zeros * (end * (ones - 1.0)))

    for at in range(0, 2 * half, TILE):
        value = jnp.broadcast_to(first_term, (TILE, width))
        for k in range(knots):
            value = value + (
                waves[k, 0, at:at + TILE, :] * coef[knots + k:knots + k + 1, :]
                - waves[k, 1, at:at + TILE, :] * coef[k:k + 1, :]
            )
        grads[at:at + TILE, :] = value.astype(jnp.bfloat16)

    columns = depth // PARTS

    def back(value, p):
        return lax.dot_general(
            value, unit[p * columns:(p + 1) * columns, :], (((1,), (1,)), ((), ())),
            preferred_element_type=jnp.float32,
        )

    both = grads[...]
    for p in range(PARTS):
        value = back(both, p)
        kept[p] = value[0:half]
        pair_out[p] = value[half:2 * half]
        remote(pair_out.at[p], pair_in.at[p], p_send, p_recv.at[p], partner).start()
    for p in range(PARTS):
        wait_all(pair_in.at[p], p_recv.at[p])
        value = kept[p] + pair_in[p]
        for c in range(chips):
            z_own[p, c] = value[c * per:(c + 1) * per]
            z_out[p, c] = to_wire(value[c * per:(c + 1) * per])
        for c in chip_peers:
            remote(
                z_out.at[p, c], z_in.at[p, chip], z_send, z_recv.at[p], (b, c * 2 + core)
            ).start()
    if nb > 1:
        wait_all(sums.at[pl.ds(0, nb - 1)], s_send)
    wait_all(pair_out, p_send)
    for p in range(PARTS):
        value = z_own[p, chip]
        if chips > 1:
            wait_all(z_in.at[p, pl.ds(0, chips - 1)], z_recv.at[p])
        for c in chip_peers:
            value = value + from_wire(z_in[p, c])
        out_ref[:, p * columns:(p + 1) * columns] = value
    if chips > 1:
        wait_all(z_out.at[:, pl.ds(0, chips - 1)], z_send)


def local(nb, nd, embeddings, directions):
    per, depth = embeddings.shape
    width = directions.shape[1]
    chips = nd // 2
    half = chips * per
    knots = KNOTS - 1
    columns = depth // PARTS
    f32, bf16 = jnp.float32, jnp.bfloat16
    dma = pltpu.SemaphoreType.DMA
    return pl.pallas_call(
        functools.partial(kernel, nb, nd),
        out_shape=jax.ShapeDtypeStruct((per, depth), f32),
        in_specs=[pl.BlockSpec(memory_space=pltpu.HBM)] * 2,
        out_specs=pl.BlockSpec(memory_space=pltpu.VMEM),
        scratch_shapes=[
            pltpu.VMEM((depth, width), bf16),
            pltpu.VMEM((depth, width), bf16),
            pltpu.VMEM((2, chips, per, depth), bf16),
            pltpu.VMEM((half, depth), f32),
            pltpu.VMEM((knots, 2, 2 * half, width), f32),
            pltpu.VMEM((width // 128, 2 * knots * 8, 128), f32),
            pltpu.VMEM((nb, 2 * knots, width), f32),
            pltpu.VMEM((2 * knots, width), f32),
            pltpu.VMEM((2 * half, width), bf16),
            pltpu.VMEM((PARTS, half, columns), f32),
            pltpu.VMEM((PARTS, half, columns), f32),
            pltpu.VMEM((PARTS, half, columns), f32),
            pltpu.VMEM((PARTS, chips, per, columns), f32),
            pltpu.VMEM((PARTS, chips, per, columns), bf16),
            pltpu.VMEM((PARTS, chips, per, columns), bf16),
            dma,
            dma,
            dma,
            dma((chips,)),
            dma,
            dma,
            dma,
            dma,
            dma,
            dma((PARTS,)),
            dma,
            dma((PARTS,)),
        ],
        compiler_params=pltpu.CompilerParams(
            collective_id=0, has_side_effects=True, vmem_limit_bytes=56 * 1000 * 1000
        ),
        name="sigreg_backward",
    )(embeddings, directions)


def solution(mesh):
    placed = (P(("batch", "dir"), None), P(None, "dir"))
    return jax.shard_map(
        functools.partial(local, mesh.shape["batch"], mesh.shape["dir"]),
        mesh=mesh, in_specs=placed, out_specs=P(("batch", "dir"), None), check_vma=False,
    )
```

```python
import functools

import jax
import jax.numpy as jnp
from jax import lax
from jax.experimental import pallas as pl
from jax.experimental.pallas import tpu as pltpu
from jax.sharding import PartitionSpec as P

KNOTS = 17
SPACING = 3.0 / (KNOTS - 1)
MESH = pl.DeviceIdType.MESH
TILE = 16
PARTS = 2
STEPS = 8
LIFT = 2.0 ** 50


def to_wire(value):
    value = value * LIFT
    return (value * jnp.abs(value)).astype(jnp.bfloat16)


def from_wire(value):
    value = value.astype(jnp.float32)
    return value * lax.rsqrt(jnp.maximum(jnp.abs(value), 2.0 ** -126)) * (1.0 / LIFT)


def sin_cos(angle):
    n = jnp.round(angle * 0.15915494309189535)
    rest = ((angle - n * 6.28125) - n * 1.9350051879882812e-3) - n * 3.019915981956753e-7
    rest = rest * 0.25
    z = rest * rest
    sine = rest + rest * z * (-1.6666654611e-1 + z * (8.3321608736e-3 - z * 1.9515295891e-4))
    cosine = 1.0 - 0.5 * z + z * z * (
        4.166664568298827e-2 + z * (-1.388731625493765e-3 + z * 2.443315711809948e-5)
    )
    for _ in range(2):
        twice = sine + sine
        sine, cosine = twice * cosine, 1.0 - twice * sine
    return sine, cosine


def kernel(
    nb, nd, emb_ref, dir_ref, out_ref,
    raw, unit, blocks, rows_f32, waves, acc, sums, coef, grads,
    kept, pair_out, pair_in, z_own, z_out, z_in,
    raw_sem, own_sem, e_send, e_recv, f_send, f_recv, s_send, s_recv, p_send, p_recv, z_send, z_recv,
):
    chips = nd // 2
    half = chips * emb_ref.shape[0]
    per = emb_ref.shape[0]
    depth = raw.shape[0]
    total_rows = half * 2 * nb
    b, d = lax.axis_index("batch"), lax.axis_index("dir")
    chip, core = d // 2, lax.rem(d, 2)
    other = 1 - core
    partner = (b, chip * 2 + other)
    step_rows = depth // STEPS

    def remote(src, dst, send_sem, recv_sem, device):
        return pltpu.make_async_remote_copy(
            src_ref=src, dst_ref=dst, send_sem=send_sem, recv_sem=recv_sem,
            device_id=device, device_id_type=MESH,
        )

    def wait_all(ref, sem):
        pltpu.make_async_copy(ref, ref, sem).wait()

    load = pltpu.make_async_copy(dir_ref, raw, raw_sem)
    load.start()
    own = pltpu.make_async_copy(emb_ref, blocks.at[core, chip], own_sem)
    own.start()

    upper = (2 * chip) // chips
    near_end = upper * chip + (1 - upper) * (chips - 1 - chip)
    chip_peers = []
    for j in range(chips - 1):
        c = j + (j + chips - near_end) // chips
        chip_peers.append(upper * c + (1 - upper) * (chips - 1 - c))
    mirror = nb - 1 - b
    own_at = (b + nb - mirror) % nb
    batch_peers = [
        (mirror + j + (j + nb - own_at) // nb) % nb for j in range(nb - 1)
    ]
    barrier = pltpu.get_barrier_semaphore()
    for c in chip_peers:
        pl.semaphore_signal(barrier, inc=1, device_id=(b, c * 2 + core), device_id_type=MESH)
    for a in batch_peers:
        pl.semaphore_signal(barrier, inc=1, device_id=(a, d), device_id_type=MESH)
    pl.semaphore_signal(barrier, inc=1, device_id=partner, device_id_type=MESH)
    pl.semaphore_wait(barrier, len(chip_peers) + len(batch_peers) + 1)

    mine = blocks.at[core, chip]
    own.wait()
    for c in chip_peers:
        remote(mine, mine, e_send, e_recv.at[chip], (b, c * 2 + core)).start()
    remote(mine, mine, e_send, f_recv, partner).start()

    load.wait()
    width = raw.shape[1]

    def add_squares(i, square):
        part = pl.ds(pl.multiple_of(i * step_rows, step_rows), step_rows)
        value = raw[part, :].astype(jnp.float32)
        return square + jnp.sum((value * value).reshape(step_rows // 8, 8, width), axis=0)

    square = lax.fori_loop(0, STEPS, add_squares, jnp.zeros((8, width), jnp.float32))
    scale = 1.0 / jnp.sqrt(jnp.sum(square, axis=0, keepdims=True) + 1e-06)

    def normalize(i, carry):
        part = pl.ds(pl.multiple_of(i * step_rows, step_rows), step_rows)
        unit[part, :] = (raw[part, :].astype(jnp.float32) * scale).astype(jnp.bfloat16)
        return carry

    lax.fori_loop(0, STEPS, normalize, 0)

    for c in reversed(chip_peers):
        block = blocks.at[core, c]
        remote(block, block, f_send, e_recv.at[c], partner).wait_recv()
        remote(block, block, f_send, f_recv, partner).start()

    knots = KNOTS - 1

    def project(side):
        for c in range(chips):
            rows_f32[c * per:(c + 1) * per, :] = blocks[side, c].astype(jnp.float32)
        return jnp.dot(
            rows_f32[...].astype(jnp.bfloat16), unit[...], preferred_element_type=jnp.float32
        )

    def fold(value):
        return jnp.sum(value.reshape(TILE // 8, 8, -1), axis=0)

    def trig(which, projected):
        for r in range(half // TILE):
            at = r * TILE
            sine1, cosine1 = sin_cos(SPACING * projected[r * TILE:(r + 1) * TILE])
            powers = {1: (cosine1, sine1)}
            for k in range(1, KNOTS):
                if k > 1 and k % 2 == 0:
                    cosine, sine = powers[k // 2]
                    twice = cosine + cosine
                    powers[k] = (twice * cosine - 1.0, twice * sine)
                elif k > 1:
                    (cos_a, sin_a), (cos_b, sin_b) = powers[k // 2], powers[k // 2 + 1]
                    powers[k] = (cos_a * cos_b - sin_a * sin_b, sin_a * cos_b + cos_a * sin_b)
                for s in range(2):
                    waves[k - 1, s, which, at:at + TILE, :] = powers[k][s]
                    part = fold(powers[k][s])
                    rows = pl.ds((s * knots + k - 1) * 8, 8)
                    for v in range(width // 128):
                        piece = part[:, v * 128:(v + 1) * 128]
                        acc[v, rows, :] += piece

    acc[...] = jnp.zeros_like(acc)

    def stage(which, carry):
        @pl.when(which == 1)
        def _():
            wait_all(blocks.at[other], f_recv)

        trig(which, project(lax.rem(core + which, 2)))
        return carry

    lax.fori_loop(0, 2, stage, 0)
    for v in range(width // 128):
        value = acc[v, pl.ds(0, 2 * knots, stride=8), :]
        for i in range(1, 8):
            value = value + acc[v, pl.ds(i, 2 * knots, stride=8), :]
        sums[b, :, v * 128:(v + 1) * 128] = value
    for a in batch_peers:
        remote(sums.at[b], sums.at[b], s_send, s_recv, (a, d)).start()

    knot = lax.broadcasted_iota(jnp.int32, (knots, width), 0).astype(jnp.float32) + 1.0
    pos = knot * SPACING
    target = jnp.exp(-0.5 * pos * pos)
    ends = jnp.where(knot == float(knots), 0.5, 1.0)
    weight = 2.0 * (ends * SPACING * target)
    wait_all(blocks.at[0], e_send)
    if chips > 1:
        wait_all(blocks.at[0, pl.ds(0, chips - 1)], f_send)
    if nb > 1:
        wait_all(sums.at[pl.ds(0, nb - 1)], s_recv)
    total = sums[0]
    for a in range(1, nb):
        total = total + sums[a]
    mean = total * (1.0 / total_rows)
    coef[0:knots, :] = pos * (weight * (mean[0:knots] - target))
    coef[knots:2 * knots, :] = pos * (weight * mean[knots:2 * knots])
    ones = jnp.full((1, width), 1.0, jnp.float32)
    zeros = jnp.zeros((1, width), jnp.float32)
    end = 2.0 * 0.5 * SPACING
    first_term = 0.0 * (ones * (end * zeros) - zeros * (end * (ones - 1.0)))

    for tile in range(2 * half // TILE):
        at = tile * TILE
        which, start = at // half, at % half
        value = jnp.broadcast_to(first_term, (TILE, width))
        for k in range(knots):
            value = value + (
                waves[k, 0, which, start:start + TILE, :] * coef[knots + k:knots + k + 1, :]
                - waves[k, 1, which, start:start + TILE, :] * coef[k:k + 1, :]
            )
        grads[at:at + TILE, :] = value.astype(jnp.bfloat16)

    columns = depth // PARTS

    def back(value, p):
        return lax.dot_general(
            value, unit[pl.ds(pl.multiple_of(p * columns, columns), columns), :], (((1,), (1,)), ((), ())),
            preferred_element_type=jnp.float32,
        )

    both = grads[...]

    def back_part(p, carry):
        value = back(both, p)
        kept[p] = value[0:half]
        pair_out[p] = value[half:2 * half]
        remote(pair_out.at[p], pair_in.at[p], p_send, p_recv.at[p], partner).start()
        return carry

    lax.fori_loop(0, PARTS, back_part, 0)
    for p in range(PARTS):
        wait_all(pair_in.at[p], p_recv.at[p])
        value = kept[p] + pair_in[p]
        for c in range(chips):
            z_own[p, c] = value[c * per:(c + 1) * per]
            z_out[p, c] = to_wire(value[c * per:(c + 1) * per])
        for c in chip_peers:
            remote(
                z_out.at[p, c], z_in.at[p, chip], z_send, z_recv.at[p], (b, c * 2 + core)
            ).start()
    if nb > 1:
        wait_all(sums.at[pl.ds(0, nb - 1)], s_send)
    wait_all(pair_out, p_send)
    for p in range(PARTS):
        value = z_own[p, chip]
        if chips > 1:
            wait_all(z_in.at[p, pl.ds(0, chips - 1)], z_recv.at[p])
        for c in chip_peers:
            value = value + from_wire(z_in[p, c])
        out_ref[:, p * columns:(p + 1) * columns] = value
    if chips > 1:
        wait_all(z_out.at[:, pl.ds(0, chips - 1)], z_send)


def local(nb, nd, embeddings, directions):
    per, depth = embeddings.shape
    width = directions.shape[1]
    chips = nd // 2
    half = chips * per
    knots = KNOTS - 1
    columns = depth // PARTS
    f32, bf16 = jnp.float32, jnp.bfloat16
    dma = pltpu.SemaphoreType.DMA
    return pl.pallas_call(
        functools.partial(kernel, nb, nd),
        out_shape=jax.ShapeDtypeStruct((per, depth), f32),
        in_specs=[pl.BlockSpec(memory_space=pltpu.HBM)] * 2,
        out_specs=pl.BlockSpec(memory_space=pltpu.VMEM),
        scratch_shapes=[
            pltpu.VMEM((depth, width), bf16),
            pltpu.VMEM((depth, width), bf16),
            pltpu.VMEM((2, chips, per, depth), bf16),
            pltpu.VMEM((half, depth), f32),
            pltpu.VMEM((knots, 2, 2, half, width), f32),
            pltpu.VMEM((width // 128, 2 * knots * 8, 128), f32),
            pltpu.VMEM((nb, 2 * knots, width), f32),
            pltpu.VMEM((2 * knots, width), f32),
            pltpu.VMEM((2 * half, width), bf16),
            pltpu.VMEM((PARTS, half, columns), f32),
            pltpu.VMEM((PARTS, half, columns), f32),
            pltpu.VMEM((PARTS, half, columns), f32),
            pltpu.VMEM((PARTS, chips, per, columns), f32),
            pltpu.VMEM((PARTS, chips, per, columns), bf16),
            pltpu.VMEM((PARTS, chips, per, columns), bf16),
            dma,
            dma,
            dma,
            dma((chips,)),
            dma,
            dma,
            dma,
            dma,
            dma,
            dma((PARTS,)),
            dma,
            dma((PARTS,)),
        ],
        compiler_params=pltpu.CompilerParams(
            collective_id=0, has_side_effects=True, vmem_limit_bytes=56 * 1000 * 1000
        ),
        name="sigreg_backward",
    )(embeddings, directions)


def solution(mesh):
    placed = (P(("batch", "dir"), None), P(None, "dir"))
    return jax.shard_map(
        functools.partial(local, mesh.shape["batch"], mesh.shape["dir"]),
        mesh=mesh, in_specs=placed, out_specs=P(("batch", "dir"), None), check_vma=False,
    )
```

```python
import functools

import jax
import jax.numpy as jnp
from jax import lax
from jax.experimental import pallas as pl
from jax.experimental.pallas import tpu as pltpu
from jax.sharding import PartitionSpec as P

KNOTS = 17
SPACING = 3.0 / (KNOTS - 1)
MESH = pl.DeviceIdType.MESH
TILE = 16
PARTS = 2
STEPS = 8
LIFT = 2.0 ** 50


def to_wire(value):
    value = value * LIFT
    return (value * jnp.abs(value)).astype(jnp.bfloat16)


def from_wire(value):
    value = value.astype(jnp.float32)
    return value * lax.rsqrt(jnp.maximum(jnp.abs(value), 2.0 ** -126)) * (1.0 / LIFT)


def sin_cos(angle):
    n = jnp.round(angle * 0.15915494309189535)
    rest = ((angle - n * 6.28125) - n * 1.9350051879882812e-3) - n * 3.019915981956753e-7
    rest = rest * 0.25
    z = rest * rest
    sine = rest + rest * z * (-1.6666654611e-1 + z * (8.3321608736e-3 - z * 1.9515295891e-4))
    cosine = 1.0 - 0.5 * z + z * z * (
        4.166664568298827e-2 + z * (-1.388731625493765e-3 + z * 2.443315711809948e-5)
    )
    for _ in range(2):
        twice = sine + sine
        sine, cosine = twice * cosine, 1.0 - twice * sine
    return sine, cosine


def kernel(
    nb, nd, emb_ref, dir_ref, out_ref,
    raw, unit, blocks, rows_f32, waves, acc, sums, coef, grads,
    kept, pair_out, pair_in, z_own, z_out, z_in,
    raw_sem, own_sem, e_send, e_recv, f_send, f_recv, s_send, s_recv, p_send, p_recv, z_send, z_recv,
):
    chips = nd // 2
    half = chips * emb_ref.shape[0]
    per = emb_ref.shape[0]
    depth = raw.shape[0]
    total_rows = half * 2 * nb
    b, d = lax.axis_index("batch"), lax.axis_index("dir")
    chip, core = d // 2, lax.rem(d, 2)
    other = 1 - core
    partner = (b, chip * 2 + other)
    step_rows = depth // STEPS

    def remote(src, dst, send_sem, recv_sem, device):
        return pltpu.make_async_remote_copy(
            src_ref=src, dst_ref=dst, send_sem=send_sem, recv_sem=recv_sem,
            device_id=device, device_id_type=MESH,
        )

    def wait_all(ref, sem):
        pltpu.make_async_copy(ref, ref, sem).wait()

    load = pltpu.make_async_copy(dir_ref, raw, raw_sem)
    load.start()
    own = pltpu.make_async_copy(emb_ref, blocks.at[core, chip], own_sem)
    own.start()

    upper = (2 * chip) // chips
    near_end = upper * chip + (1 - upper) * (chips - 1 - chip)
    chip_peers = []
    for j in range(chips - 1):
        c = j + (j + chips - near_end) // chips
        chip_peers.append(upper * c + (1 - upper) * (chips - 1 - c))
    mirror = nb - 1 - b
    own_at = (b + nb - mirror) % nb
    batch_peers = [
        (mirror + j + (j + nb - own_at) // nb) % nb for j in range(nb - 1)
    ]
    barrier = pltpu.get_barrier_semaphore()
    for c in chip_peers:
        pl.semaphore_signal(barrier, inc=1, device_id=(b, c * 2 + core), device_id_type=MESH)
    for a in batch_peers:
        pl.semaphore_signal(barrier, inc=1, device_id=(a, d), device_id_type=MESH)
    pl.semaphore_signal(barrier, inc=1, device_id=partner, device_id_type=MESH)
    pl.semaphore_wait(barrier, len(chip_peers) + len(batch_peers) + 1)

    mine = blocks.at[core, chip]
    own.wait()
    for c in chip_peers:
        remote(mine, mine, e_send, e_recv.at[chip], (b, c * 2 + core)).start()
    remote(mine, mine, e_send, f_recv, partner).start()

    load.wait()
    width = raw.shape[1]

    def add_squares(i, square):
        part = pl.ds(pl.multiple_of(i * step_rows, step_rows), step_rows)
        value = raw[part, :].astype(jnp.float32)
        return square + jnp.sum((value * value).reshape(step_rows // 8, 8, width), axis=0)

    square = lax.fori_loop(0, STEPS, add_squares, jnp.zeros((8, width), jnp.float32))
    scale = 1.0 / jnp.sqrt(jnp.sum(square, axis=0, keepdims=True) + 1e-06)

    def normalize(i, carry):
        part = pl.ds(pl.multiple_of(i * step_rows, step_rows), step_rows)
        unit[part, :] = (raw[part, :].astype(jnp.float32) * scale).astype(jnp.bfloat16)
        return carry

    lax.fori_loop(0, STEPS, normalize, 0)

    for c in reversed(chip_peers):
        block = blocks.at[core, c]
        remote(block, block, f_send, e_recv.at[c], partner).wait_recv()
        remote(block, block, f_send, f_recv, partner).start()

    knots = KNOTS - 1

    def project(side):
        for c in range(chips):
            rows_f32[c * per:(c + 1) * per, :] = blocks[side, c].astype(jnp.float32)
        return jnp.dot(
            rows_f32[...].astype(jnp.bfloat16), unit[...], preferred_element_type=jnp.float32
        )

    def fold(value):
        return jnp.sum(value.reshape(TILE // 8, 8, -1), axis=0)

    def trig(which, projected):
        for r in range(half // TILE):
            at = r * TILE
            sine1, cosine1 = sin_cos(SPACING * projected[r * TILE:(r + 1) * TILE])
            powers = {1: (cosine1, sine1)}
            for k in range(1, KNOTS):
                if k > 1 and k % 2 == 0:
                    cosine, sine = powers[k // 2]
                    twice = cosine + cosine
                    powers[k] = (twice * cosine - 1.0, twice * sine)
                elif k > 1:
                    (cos_a, sin_a), (cos_b, sin_b) = powers[k // 2], powers[k // 2 + 1]
                    powers[k] = (cos_a * cos_b - sin_a * sin_b, sin_a * cos_b + cos_a * sin_b)
                for s in range(2):
                    waves[k - 1, s, which, at:at + TILE, :] = powers[k][s]
                    part = fold(powers[k][s])
                    rows = pl.ds((s * knots + k - 1) * 8, 8)
                    for v in range(width // 128):
                        piece = part[:, v * 128:(v + 1) * 128]
                        acc[v, rows, :] += piece

    acc[...] = jnp.zeros_like(acc)

    def stage(which, carry):
        @pl.when(which == 1)
        def _():
            wait_all(blocks.at[other], f_recv)

        trig(which, project(lax.rem(core + which, 2)))
        return carry

    lax.fori_loop(0, 2, stage, 0)
    for v in range(width // 128):
        value = acc[v, pl.ds(0, 2 * knots, stride=8), :]
        for i in range(1, 8):
            value = value + acc[v, pl.ds(i, 2 * knots, stride=8), :]
        sums[b, :, v * 128:(v + 1) * 128] = value
    for a in batch_peers:
        remote(sums.at[b], sums.at[b], s_send, s_recv, (a, d)).start()

    knot = lax.broadcasted_iota(jnp.int32, (knots, width), 0).astype(jnp.float32) + 1.0
    pos = knot * SPACING
    target = jnp.exp(-0.5 * pos * pos)
    ends = jnp.where(knot == float(knots), 0.5, 1.0)
    weight = 2.0 * (ends * SPACING * target)
    wait_all(blocks.at[0], e_send)
    if chips > 1:
        wait_all(blocks.at[0, pl.ds(0, chips - 1)], f_send)
    if nb > 1:
        wait_all(sums.at[pl.ds(0, nb - 1)], s_recv)
    total = sums[0]
    for a in range(1, nb):
        total = total + sums[a]
    mean = total * (1.0 / total_rows)
    coef[0:knots, :] = pos * (weight * (mean[0:knots] - target))
    coef[knots:2 * knots, :] = pos * (weight * mean[knots:2 * knots])
    ones = jnp.full((1, width), 1.0, jnp.float32)
    zeros = jnp.zeros((1, width), jnp.float32)
    end = 2.0 * 0.5 * SPACING
    first_term = 0.0 * (ones * (end * zeros) - zeros * (end * (ones - 1.0)))

    for tile in range(2 * half // TILE):
        at = tile * TILE
        which, start = at // half, at % half
        value = jnp.broadcast_to(first_term, (TILE, width))
        for k in range(knots):
            value = value + (
                waves[k, 0, which, start:start + TILE, :] * coef[knots + k:knots + k + 1, :]
                - waves[k, 1, which, start:start + TILE, :] * coef[k:k + 1, :]
            )
        grads[at:at + TILE, :] = value.astype(jnp.bfloat16)

    columns = depth // PARTS

    def back(value, p):
        return lax.dot_general(
            value, unit[pl.ds(pl.multiple_of(p * columns, columns), columns), :], (((1,), (1,)), ((), ())),
            preferred_element_type=jnp.float32,
        )

    both = grads[...]

    def back_part(p, carry):
        value = back(both, p)
        kept[p] = value[0:half]
        pair_out[p] = value[half:2 * half]
        remote(pair_out.at[p], pair_in.at[p], p_send, p_recv.at[p], partner).start()
        return carry

    lax.fori_loop(0, PARTS, back_part, 0)
    for p in range(PARTS):
        wait_all(pair_in.at[p], p_recv.at[p])
        value = kept[p] + pair_in[p]
        for c in range(chips):
            z_own[p, c] = value[c * per:(c + 1) * per]
            z_out[p, c] = to_wire(value[c * per:(c + 1) * per])
        for c in chip_peers:
            remote(
                z_out.at[p, c], z_in.at[p, chip], z_send, z_recv.at[p], (b, c * 2 + core)
            ).start()
    if nb > 1:
        wait_all(sums.at[pl.ds(0, nb - 1)], s_send)
    wait_all(pair_out, p_send)
    for p in range(PARTS):
        value = z_own[p, chip]
        if chips > 1:
            wait_all(z_in.at[p, pl.ds(0, chips - 1)], z_recv.at[p])
        for c in chip_peers:
            value = value + from_wire(z_in[p, c])
        out_ref[:, p * columns:(p + 1) * columns] = value
    if chips > 1:
        wait_all(z_out.at[:, pl.ds(0, chips - 1)], z_send)


def local(nb, nd, embeddings, directions):
    per, depth = embeddings.shape
    width = directions.shape[1]
    chips = nd // 2
    half = chips * per
    knots = KNOTS - 1
    columns = depth // PARTS
    f32, bf16 = jnp.float32, jnp.bfloat16
    dma = pltpu.SemaphoreType.DMA
    return pl.pallas_call(
        functools.partial(kernel, nb, nd),
        out_shape=jax.ShapeDtypeStruct((per, depth), f32),
        in_specs=[pl.BlockSpec(memory_space=pltpu.HBM)] * 2,
        out_specs=pl.BlockSpec(memory_space=pltpu.VMEM),
        scratch_shapes=[
            pltpu.VMEM((depth, width), bf16),
            pltpu.VMEM((depth, width), bf16),
            pltpu.VMEM((2, chips, per, depth), bf16),
            pltpu.VMEM((half, depth), f32),
            pltpu.VMEM((knots, 2, 2, half, width), f32),
            pltpu.VMEM((width // 128, 2 * knots * 8, 128), f32),
            pltpu.VMEM((nb, 2 * knots, width), f32),
            pltpu.VMEM((2 * knots, width), f32),
            pltpu.VMEM((2 * half, width), bf16),
            pltpu.VMEM((PARTS, half, columns), f32),
            pltpu.VMEM((PARTS, half, columns), f32),
            pltpu.VMEM((PARTS, half, columns), f32),
            pltpu.VMEM((PARTS, chips, per, columns), f32),
            pltpu.VMEM((PARTS, chips, per, columns), bf16),
            pltpu.VMEM((PARTS, chips, per, columns), bf16),
            dma,
            dma,
            dma,
            dma((chips,)),
            dma,
            dma,
            dma,
            dma,
            dma,
            dma((PARTS,)),
            dma,
            dma((PARTS,)),
        ],
        compiler_params=pltpu.CompilerParams(
            collective_id=0, has_side_effects=True, vmem_limit_bytes=56 * 1000 * 1000
        ),
        name="sigreg_backward",
    )(
        pltpu.with_memory_space_constraint(embeddings, pltpu.HBM),
        pltpu.with_memory_space_constraint(directions, pltpu.HBM),
    )


def solution(mesh):
    placed = (P(("batch", "dir"), None), P(None, "dir"))
    return jax.shard_map(
        functools.partial(local, mesh.shape["batch"], mesh.shape["dir"]),
        mesh=mesh, in_specs=placed, out_specs=P(("batch", "dir"), None), check_vma=False,
    )
```

```python
import functools

import jax
import jax.numpy as jnp
from jax import lax
from jax.experimental import pallas as pl
from jax.experimental.pallas import tpu as pltpu
from jax.sharding import PartitionSpec as P

KNOTS = 17
SPACING = 3.0 / (KNOTS - 1)
MESH = pl.DeviceIdType.MESH
TILE = 16
PARTS = 2
STEPS = 8
LIFT = 2.0 ** 50


def to_wire(value):
    value = value * LIFT
    return (value * jnp.abs(value)).astype(jnp.bfloat16)


def from_wire(value):
    value = value.astype(jnp.float32)
    return value * lax.rsqrt(jnp.maximum(jnp.abs(value), 2.0 ** -126)) * (1.0 / LIFT)


def sin_cos(angle):
    n = jnp.round(angle * 0.15915494309189535)
    rest = ((angle - n * 6.28125) - n * 1.9350051879882812e-3) - n * 3.019915981956753e-7
    rest = rest * 0.25
    z = rest * rest
    sine = rest + rest * z * (-1.6666654611e-1 + z * (8.3321608736e-3 - z * 1.9515295891e-4))
    cosine = 1.0 - 0.5 * z + z * z * (
        4.166664568298827e-2 + z * (-1.388731625493765e-3 + z * 2.443315711809948e-5)
    )
    for _ in range(2):
        twice = sine + sine
        sine, cosine = twice * cosine, 1.0 - twice * sine
    return sine, cosine


def kernel(
    nb, nd, emb_ref, dir_ref, out_ref,
    raw, unit, blocks, rows_f32, waves, acc, sums, coef, grads,
    kept, pair_out, pair_in, z_own, z_out, z_in,
    raw_sem, own_sem, e_send, e_recv, f_send, f_recv, s_send, s_recv, p_send, p_recv, z_send, z_recv,
):
    chips = nd // 2
    half = chips * emb_ref.shape[0]
    per = emb_ref.shape[0]
    depth = raw.shape[0]
    total_rows = half * 2 * nb
    b, d = lax.axis_index("batch"), lax.axis_index("dir")
    chip, core = d // 2, lax.rem(d, 2)
    other = 1 - core
    partner = (b, chip * 2 + other)
    step_rows = depth // STEPS

    def remote(src, dst, send_sem, recv_sem, device):
        return pltpu.make_async_remote_copy(
            src_ref=src, dst_ref=dst, send_sem=send_sem, recv_sem=recv_sem,
            device_id=device, device_id_type=MESH,
        )

    def wait_all(ref, sem):
        pltpu.make_async_copy(ref, ref, sem).wait()

    own = pltpu.make_async_copy(emb_ref, blocks.at[core, chip], own_sem)
    own.start()

    upper = (2 * chip) // chips
    near_end = upper * chip + (1 - upper) * (chips - 1 - chip)
    chip_peers = []
    for j in range(chips - 1):
        c = j + (j + chips - near_end) // chips
        chip_peers.append(upper * c + (1 - upper) * (chips - 1 - c))
    mirror = nb - 1 - b
    own_at = (b + nb - mirror) % nb
    batch_peers = [
        (mirror + j + (j + nb - own_at) // nb) % nb for j in range(nb - 1)
    ]
    barrier = pltpu.get_barrier_semaphore()
    for c in chip_peers:
        pl.semaphore_signal(barrier, inc=1, device_id=(b, c * 2 + core), device_id_type=MESH)
    for a in batch_peers:
        pl.semaphore_signal(barrier, inc=1, device_id=(a, d), device_id_type=MESH)
    pl.semaphore_signal(barrier, inc=1, device_id=partner, device_id_type=MESH)
    load = pltpu.make_async_copy(dir_ref, raw, raw_sem)
    load.start()
    pl.semaphore_wait(barrier, len(chip_peers) + len(batch_peers) + 1)

    mine = blocks.at[core, chip]
    own.wait()
    for c in chip_peers:
        remote(mine, mine, e_send, e_recv.at[chip], (b, c * 2 + core)).start()
    remote(mine, mine, e_send, f_recv, partner).start()

    load.wait()
    width = raw.shape[1]

    def add_squares(i, square):
        part = pl.ds(pl.multiple_of(i * step_rows, step_rows), step_rows)
        value = raw[part, :].astype(jnp.float32)
        return square + jnp.sum((value * value).reshape(step_rows // 8, 8, width), axis=0)

    square = lax.fori_loop(0, STEPS, add_squares, jnp.zeros((8, width), jnp.float32))
    scale = 1.0 / jnp.sqrt(jnp.sum(square, axis=0, keepdims=True) + 1e-06)

    def normalize(i, carry):
        part = pl.ds(pl.multiple_of(i * step_rows, step_rows), step_rows)
        unit[part, :] = (raw[part, :].astype(jnp.float32) * scale).astype(jnp.bfloat16)
        return carry

    lax.fori_loop(0, STEPS, normalize, 0)

    for c in reversed(chip_peers):
        block = blocks.at[core, c]
        remote(block, block, f_send, e_recv.at[c], partner).wait_recv()
        remote(block, block, f_send, f_recv, partner).start()

    knots = KNOTS - 1

    def project(side):
        for c in range(chips):
            rows_f32[c * per:(c + 1) * per, :] = blocks[side, c].astype(jnp.float32)
        return jnp.dot(
            rows_f32[...].astype(jnp.bfloat16), unit[...], preferred_element_type=jnp.float32
        )

    def fold(value):
        return jnp.sum(value.reshape(TILE // 8, 8, -1), axis=0)

    def trig(which, projected):
        for r in range(half // TILE):
            at = r * TILE
            sine1, cosine1 = sin_cos(SPACING * projected[r * TILE:(r + 1) * TILE])
            powers = {1: (cosine1, sine1)}
            for k in range(1, KNOTS):
                if k > 1 and k % 2 == 0:
                    cosine, sine = powers[k // 2]
                    twice = cosine + cosine
                    powers[k] = (twice * cosine - 1.0, twice * sine)
                elif k > 1:
                    (cos_a, sin_a), (cos_b, sin_b) = powers[k // 2], powers[k // 2 + 1]
                    powers[k] = (cos_a * cos_b - sin_a * sin_b, sin_a * cos_b + cos_a * sin_b)
                for s in range(2):
                    waves[k - 1, s, which, at:at + TILE, :] = powers[k][s]
                    part = fold(powers[k][s])
                    rows = pl.ds((s * knots + k - 1) * 8, 8)
                    for v in range(width // 128):
                        piece = part[:, v * 128:(v + 1) * 128]
                        acc[v, rows, :] += piece

    acc[...] = jnp.zeros_like(acc)

    def stage(which, carry):
        @pl.when(which == 1)
        def _():
            wait_all(blocks.at[other], f_recv)

        trig(which, project(lax.rem(core + which, 2)))
        return carry

    lax.fori_loop(0, 2, stage, 0)
    for v in range(width // 128):
        value = acc[v, pl.ds(0, 2 * knots, stride=8), :]
        for i in range(1, 8):
            value = value + acc[v, pl.ds(i, 2 * knots, stride=8), :]
        sums[b, :, v * 128:(v + 1) * 128] = value
    for a in batch_peers:
        remote(sums.at[b], sums.at[b], s_send, s_recv, (a, d)).start()

    knot = lax.broadcasted_iota(jnp.int32, (knots, width), 0).astype(jnp.float32) + 1.0
    pos = knot * SPACING
    target = jnp.exp(-0.5 * pos * pos)
    ends = jnp.where(knot == float(knots), 0.5, 1.0)
    weight = 2.0 * (ends * SPACING * target)
    wait_all(blocks.at[0], e_send)
    if chips > 1:
        wait_all(blocks.at[0, pl.ds(0, chips - 1)], f_send)
    if nb > 1:
        wait_all(sums.at[pl.ds(0, nb - 1)], s_recv)
    total = sums[0]
    for a in range(1, nb):
        total = total + sums[a]
    mean = total * (1.0 / total_rows)
    coef[0:knots, :] = pos * (weight * (mean[0:knots] - target))
    coef[knots:2 * knots, :] = pos * (weight * mean[knots:2 * knots])
    ones = jnp.full((1, width), 1.0, jnp.float32)
    zeros = jnp.zeros((1, width), jnp.float32)
    end = 2.0 * 0.5 * SPACING
    first_term = 0.0 * (ones * (end * zeros) - zeros * (end * (ones - 1.0)))

    for tile in range(2 * half // TILE):
        at = tile * TILE
        which, start = at // half, at % half
        value = jnp.broadcast_to(first_term, (TILE, width))
        for k in range(knots):
            value = value + (
                waves[k, 0, which, start:start + TILE, :] * coef[knots + k:knots + k + 1, :]
                - waves[k, 1, which, start:start + TILE, :] * coef[k:k + 1, :]
            )
        grads[at:at + TILE, :] = value.astype(jnp.bfloat16)

    columns = depth // PARTS

    def back(value, p):
        return lax.dot_general(
            value, unit[pl.ds(pl.multiple_of(p * columns, columns), columns), :], (((1,), (1,)), ((), ())),
            preferred_element_type=jnp.float32,
        )

    both = grads[...]

    def back_part(p, carry):
        value = back(both, p)
        kept[p] = value[0:half]
        pair_out[p] = value[half:2 * half]
        remote(pair_out.at[p], pair_in.at[p], p_send, p_recv.at[p], partner).start()
        return carry

    lax.fori_loop(0, PARTS, back_part, 0)
    for p in range(PARTS):
        wait_all(pair_in.at[p], p_recv.at[p])
        value = kept[p] + pair_in[p]
        for c in range(chips):
            z_own[p, c] = value[c * per:(c + 1) * per]
            z_out[p, c] = to_wire(value[c * per:(c + 1) * per])
        for c in chip_peers:
            remote(
                z_out.at[p, c], z_in.at[p, chip], z_send, z_recv.at[p], (b, c * 2 + core)
            ).start()
    if nb > 1:
        wait_all(sums.at[pl.ds(0, nb - 1)], s_send)
    wait_all(pair_out, p_send)
    for p in range(PARTS):
        value = z_own[p, chip]
        if chips > 1:
            wait_all(z_in.at[p, pl.ds(0, chips - 1)], z_recv.at[p])
        for c in chip_peers:
            value = value + from_wire(z_in[p, c])
        out_ref[:, p * columns:(p + 1) * columns] = value
    if chips > 1:
        wait_all(z_out.at[:, pl.ds(0, chips - 1)], z_send)


def local(nb, nd, embeddings, directions):
    per, depth = embeddings.shape
    width = directions.shape[1]
    chips = nd // 2
    half = chips * per
    knots = KNOTS - 1
    columns = depth // PARTS
    f32, bf16 = jnp.float32, jnp.bfloat16
    dma = pltpu.SemaphoreType.DMA
    return pl.pallas_call(
        functools.partial(kernel, nb, nd),
        out_shape=jax.ShapeDtypeStruct((per, depth), f32),
        in_specs=[pl.BlockSpec(memory_space=pltpu.HBM)] * 2,
        out_specs=pl.BlockSpec(memory_space=pltpu.VMEM),
        scratch_shapes=[
            pltpu.VMEM((depth, width), bf16),
            pltpu.VMEM((depth, width), bf16),
            pltpu.VMEM((2, chips, per, depth), bf16),
            pltpu.VMEM((half, depth), f32),
            pltpu.VMEM((knots, 2, 2, half, width), f32),
            pltpu.VMEM((width // 128, 2 * knots * 8, 128), f32),
            pltpu.VMEM((nb, 2 * knots, width), f32),
            pltpu.VMEM((2 * knots, width), f32),
            pltpu.VMEM((2 * half, width), bf16),
            pltpu.VMEM((PARTS, half, columns), f32),
            pltpu.VMEM((PARTS, half, columns), f32),
            pltpu.VMEM((PARTS, half, columns), f32),
            pltpu.VMEM((PARTS, chips, per, columns), f32),
            pltpu.VMEM((PARTS, chips, per, columns), bf16),
            pltpu.VMEM((PARTS, chips, per, columns), bf16),
            dma,
            dma,
            dma,
            dma((chips,)),
            dma,
            dma,
            dma,
            dma,
            dma,
            dma((PARTS,)),
            dma,
            dma((PARTS,)),
        ],
        compiler_params=pltpu.CompilerParams(
            collective_id=0, has_side_effects=True, vmem_limit_bytes=56 * 1000 * 1000
        ),
        name="sigreg_backward",
    )(
        pltpu.with_memory_space_constraint(embeddings, pltpu.HBM),
        pltpu.with_memory_space_constraint(directions, pltpu.HBM),
    )


def solution(mesh):
    placed = (P(("batch", "dir"), None), P(None, "dir"))
    return jax.shard_map(
        functools.partial(local, mesh.shape["batch"], mesh.shape["dir"]),
        mesh=mesh, in_specs=placed, out_specs=P(("batch", "dir"), None), check_vma=False,
    )
```

```python
import functools

import jax
import jax.numpy as jnp
from jax import lax
from jax.experimental import pallas as pl
from jax.experimental.pallas import tpu as pltpu
from jax.sharding import PartitionSpec as P

KNOTS = 17
SPACING = 3.0 / (KNOTS - 1)
MESH = pl.DeviceIdType.MESH
TILE = 16
PARTS = 4
STEPS = 8
LIFT = 2.0 ** 50


def to_wire(value):
    value = value * LIFT
    return (value * jnp.abs(value)).astype(jnp.bfloat16)


def from_wire(value):
    value = value.astype(jnp.float32)
    return value * lax.rsqrt(jnp.maximum(jnp.abs(value), 2.0 ** -126)) * (1.0 / LIFT)


def sin_cos(angle):
    n = jnp.round(angle * 0.15915494309189535)
    rest = ((angle - n * 6.28125) - n * 1.9350051879882812e-3) - n * 3.019915981956753e-7
    rest = rest * 0.25
    z = rest * rest
    sine = rest + rest * z * (-1.6666654611e-1 + z * (8.3321608736e-3 - z * 1.9515295891e-4))
    cosine = 1.0 - 0.5 * z + z * z * (
        4.166664568298827e-2 + z * (-1.388731625493765e-3 + z * 2.443315711809948e-5)
    )
    for _ in range(2):
        twice = sine + sine
        sine, cosine = twice * cosine, 1.0 - twice * sine
    return sine, cosine


def kernel(
    nb, nd, emb_ref, dir_ref, out_ref,
    raw, unit, blocks, rows_f32, waves, acc, sums, coef, grads,
    kept, pair_out, pair_in, z_own, z_out, z_in,
    raw_sem, own_sem, e_send, e_recv, f_send, f_recv, s_send, s_recv, p_send, p_recv, z_send, z_recv,
):
    chips = nd // 2
    half = chips * emb_ref.shape[0]
    per = emb_ref.shape[0]
    depth = raw.shape[0]
    total_rows = half * 2 * nb
    b, d = lax.axis_index("batch"), lax.axis_index("dir")
    chip, core = d // 2, lax.rem(d, 2)
    other = 1 - core
    partner = (b, chip * 2 + other)
    step_rows = depth // STEPS

    def remote(src, dst, send_sem, recv_sem, device):
        return pltpu.make_async_remote_copy(
            src_ref=src, dst_ref=dst, send_sem=send_sem, recv_sem=recv_sem,
            device_id=device, device_id_type=MESH,
        )

    def wait_all(ref, sem):
        pltpu.make_async_copy(ref, ref, sem).wait()

    own = pltpu.make_async_copy(emb_ref, blocks.at[core, chip], own_sem)
    own.start()

    upper = (2 * chip) // chips
    near_end = upper * chip + (1 - upper) * (chips - 1 - chip)
    chip_peers = []
    for j in range(chips - 1):
        c = j + (j + chips - near_end) // chips
        chip_peers.append(upper * c + (1 - upper) * (chips - 1 - c))
    mirror = nb - 1 - b
    own_at = (b + nb - mirror) % nb
    batch_peers = [
        (mirror + j + (j + nb - own_at) // nb) % nb for j in range(nb - 1)
    ]
    barrier = pltpu.get_barrier_semaphore()
    for c in chip_peers:
        pl.semaphore_signal(barrier, inc=1, device_id=(b, c * 2 + core), device_id_type=MESH)
    for a in batch_peers:
        pl.semaphore_signal(barrier, inc=1, device_id=(a, d), device_id_type=MESH)
    pl.semaphore_signal(barrier, inc=1, device_id=partner, device_id_type=MESH)
    load = pltpu.make_async_copy(dir_ref, raw, raw_sem)
    load.start()
    pl.semaphore_wait(barrier, len(chip_peers) + len(batch_peers) + 1)

    mine = blocks.at[core, chip]
    own.wait()
    for c in chip_peers:
        remote(mine, mine, e_send, e_recv.at[chip], (b, c * 2 + core)).start()
    remote(mine, mine, e_send, f_recv, partner).start()

    load.wait()
    width = raw.shape[1]

    def add_squares(i, square):
        part = pl.ds(pl.multiple_of(i * step_rows, step_rows), step_rows)
        value = raw[part, :].astype(jnp.float32)
        return square + jnp.sum((value * value).reshape(step_rows // 8, 8, width), axis=0)

    square = lax.fori_loop(0, STEPS, add_squares, jnp.zeros((8, width), jnp.float32))
    scale = 1.0 / jnp.sqrt(jnp.sum(square, axis=0, keepdims=True) + 1e-06)

    def normalize(i, carry):
        part = pl.ds(pl.multiple_of(i * step_rows, step_rows), step_rows)
        unit[part, :] = (raw[part, :].astype(jnp.float32) * scale).astype(jnp.bfloat16)
        return carry

    lax.fori_loop(0, STEPS, normalize, 0)

    for c in reversed(chip_peers):
        block = blocks.at[core, c]
        remote(block, block, f_send, e_recv.at[c], partner).wait_recv()
        remote(block, block, f_send, f_recv, partner).start()

    knots = KNOTS - 1

    def project(side):
        for c in range(chips):
            rows_f32[c * per:(c + 1) * per, :] = blocks[side, c].astype(jnp.float32)
        return jnp.dot(
            rows_f32[...].astype(jnp.bfloat16), unit[...], preferred_element_type=jnp.float32
        )

    def fold(value):
        return jnp.sum(value.reshape(TILE // 8, 8, -1), axis=0)

    def trig(which, projected):
        for r in range(half // TILE):
            at = r * TILE
            sine1, cosine1 = sin_cos(SPACING * projected[r * TILE:(r + 1) * TILE])
            powers = {1: (cosine1, sine1)}
            for k in range(1, KNOTS):
                if k > 1 and k % 2 == 0:
                    cosine, sine = powers[k // 2]
                    twice = cosine + cosine
                    powers[k] = (twice * cosine - 1.0, twice * sine)
                elif k > 1:
                    (cos_a, sin_a), (cos_b, sin_b) = powers[k // 2], powers[k // 2 + 1]
                    powers[k] = (cos_a * cos_b - sin_a * sin_b, sin_a * cos_b + cos_a * sin_b)
                for s in range(2):
                    waves[k - 1, s, which, at:at + TILE, :] = powers[k][s]
                    part = fold(powers[k][s])
                    rows = pl.ds((s * knots + k - 1) * 8, 8)
                    for v in range(width // 128):
                        piece = part[:, v * 128:(v + 1) * 128]
                        acc[v, rows, :] += piece

    acc[...] = jnp.zeros_like(acc)

    def stage(which, carry):
        @pl.when(which == 1)
        def _():
            wait_all(blocks.at[other], f_recv)

        trig(which, project(lax.rem(core + which, 2)))
        return carry

    lax.fori_loop(0, 2, stage, 0)
    for v in range(width // 128):
        value = acc[v, pl.ds(0, 2 * knots, stride=8), :]
        for i in range(1, 8):
            value = value + acc[v, pl.ds(i, 2 * knots, stride=8), :]
        sums[b, :, v * 128:(v + 1) * 128] = value
    for a in batch_peers:
        remote(sums.at[b], sums.at[b], s_send, s_recv, (a, d)).start()

    knot = lax.broadcasted_iota(jnp.int32, (knots, width), 0).astype(jnp.float32) + 1.0
    pos = knot * SPACING
    target = jnp.exp(-0.5 * pos * pos)
    ends = jnp.where(knot == float(knots), 0.5, 1.0)
    weight = 2.0 * (ends * SPACING * target)
    wait_all(blocks.at[0], e_send)
    if chips > 1:
        wait_all(blocks.at[0, pl.ds(0, chips - 1)], f_send)
    if nb > 1:
        wait_all(sums.at[pl.ds(0, nb - 1)], s_recv)
    total = sums[0]
    for a in range(1, nb):
        total = total + sums[a]
    mean = total * (1.0 / total_rows)
    coef[0:knots, :] = pos * (weight * (mean[0:knots] - target))
    coef[knots:2 * knots, :] = pos * (weight * mean[knots:2 * knots])
    ones = jnp.full((1, width), 1.0, jnp.float32)
    zeros = jnp.zeros((1, width), jnp.float32)
    end = 2.0 * 0.5 * SPACING
    first_term = 0.0 * (ones * (end * zeros) - zeros * (end * (ones - 1.0)))

    for tile in range(2 * half // TILE):
        at = tile * TILE
        which, start = at // half, at % half
        value = jnp.broadcast_to(first_term, (TILE, width))
        for k in range(knots):
            value = value + (
                waves[k, 0, which, start:start + TILE, :] * coef[knots + k:knots + k + 1, :]
                - waves[k, 1, which, start:start + TILE, :] * coef[k:k + 1, :]
            )
        grads[at:at + TILE, :] = value.astype(jnp.bfloat16)

    columns = depth // PARTS

    def back(value, p):
        return lax.dot_general(
            value, unit[pl.ds(pl.multiple_of(p * columns, columns), columns), :], (((1,), (1,)), ((), ())),
            preferred_element_type=jnp.float32,
        )

    both = grads[...]

    def back_part(p, carry):
        value = back(both, p)
        kept[p] = value[0:half]
        pair_out[p] = value[half:2 * half]
        remote(pair_out.at[p], pair_in.at[p], p_send, p_recv.at[p], partner).start()
        return carry

    lax.fori_loop(0, PARTS, back_part, 0)
    for p in range(PARTS):
        wait_all(pair_in.at[p], p_recv.at[p])
        value = kept[p] + pair_in[p]
        for c in range(chips):
            z_own[p, c] = value[c * per:(c + 1) * per]
            z_out[p, c] = to_wire(value[c * per:(c + 1) * per])
        for c in chip_peers:
            remote(
                z_out.at[p, c], z_in.at[p, chip], z_send, z_recv.at[p], (b, c * 2 + core)
            ).start()
    if nb > 1:
        wait_all(sums.at[pl.ds(0, nb - 1)], s_send)
    wait_all(pair_out, p_send)
    for p in range(PARTS):
        value = z_own[p, chip]
        if chips > 1:
            wait_all(z_in.at[p, pl.ds(0, chips - 1)], z_recv.at[p])
        for c in chip_peers:
            value = value + from_wire(z_in[p, c])
        out_ref[:, p * columns:(p + 1) * columns] = value
    if chips > 1:
        wait_all(z_out.at[:, pl.ds(0, chips - 1)], z_send)


def local(nb, nd, embeddings, directions):
    per, depth = embeddings.shape
    width = directions.shape[1]
    chips = nd // 2
    half = chips * per
    knots = KNOTS - 1
    columns = depth // PARTS
    f32, bf16 = jnp.float32, jnp.bfloat16
    dma = pltpu.SemaphoreType.DMA
    return pl.pallas_call(
        functools.partial(kernel, nb, nd),
        out_shape=jax.ShapeDtypeStruct((per, depth), f32),
        in_specs=[pl.BlockSpec(memory_space=pltpu.HBM)] * 2,
        out_specs=pl.BlockSpec(memory_space=pltpu.VMEM),
        scratch_shapes=[
            pltpu.VMEM((depth, width), bf16),
            pltpu.VMEM((depth, width), bf16),
            pltpu.VMEM((2, chips, per, depth), bf16),
            pltpu.VMEM((half, depth), f32),
            pltpu.VMEM((knots, 2, 2, half, width), f32),
            pltpu.VMEM((width // 128, 2 * knots * 8, 128), f32),
            pltpu.VMEM((nb, 2 * knots, width), f32),
            pltpu.VMEM((2 * knots, width), f32),
            pltpu.VMEM((2 * half, width), bf16),
            pltpu.VMEM((PARTS, half, columns), f32),
            pltpu.VMEM((PARTS, half, columns), f32),
            pltpu.VMEM((PARTS, half, columns), f32),
            pltpu.VMEM((PARTS, chips, per, columns), f32),
            pltpu.VMEM((PARTS, chips, per, columns), bf16),
            pltpu.VMEM((PARTS, chips, per, columns), bf16),
            dma,
            dma,
            dma,
            dma((chips,)),
            dma,
            dma,
            dma,
            dma,
            dma,
            dma((PARTS,)),
            dma,
            dma((PARTS,)),
        ],
        compiler_params=pltpu.CompilerParams(
            collective_id=0, has_side_effects=True, vmem_limit_bytes=56 * 1000 * 1000
        ),
        name="sigreg_backward",
    )(
        pltpu.with_memory_space_constraint(embeddings, pltpu.HBM),
        pltpu.with_memory_space_constraint(directions, pltpu.HBM),
    )


def solution(mesh):
    placed = (P(("batch", "dir"), None), P(None, "dir"))
    return jax.shard_map(
        functools.partial(local, mesh.shape["batch"], mesh.shape["dir"]),
        mesh=mesh, in_specs=placed, out_specs=P(("batch", "dir"), None), check_vma=False,
    )
```
